256 devices in a mesh: dom: 128 (over y, z, x), samp: 2 (over core).
Axes of the slice: x: 4, y: 4, z: 8, core: 2. Of those that a mesh axis runs over, the one named last changes fastest.
Arguments:
- state: float32 [2, 32768, 256], P(None, 'dom', 'samp'), may hold values from -6 to 6
- demand_load: bfloat16 [2, 256, 16384], P('samp', 'dom'), may hold values from 0.099609375 to 2
- node_coef: float32 [2, 32768], P(None, 'dom'), may hold values from 0.2 to 2
- pipe_ends: int32 [2, 65536], P(None, 'dom'), may hold values from 0 to 255, as said below
- pipe_coef: float32 [2, 65536], P(None, 'dom'), may hold values from 0.5 to 2
- iface_node: int32 [128, 4, 64], P('dom'), may hold values from 0 to 255
- iface_coef: float32 [2, 128, 2, 64], replicated, may hold values from 0.5 to 2
- cons_node: int32 [128, 256], P('dom'), may hold values from 0 to 255
- cons_count: int32 [128], P('dom'), may hold values from 1 to 256, 16384 in all
Outputs:
- newton_step: float32 [2, 32768, 256], P(None, 'dom', 'samp')
- residual: float32 [2, 32768, 256], P(None, 'dom', 'samp')
The draws below stay inside these ranges and needn't reach their ends.
Inputs may be any that keep to these rules, and one draw needn't show every extreme that they name: `pipe_ends`: the two ends of every interior pipe are different nodes of its partition.
All inputs are finite; a program needn't handle non-finite values. No bound on the sum of `cons_count` on one device may be relied on, other than what follows from the above.
Results may differ from the reference program's by a relative error of at most 0.0003.
Values may be sent and summed in bfloat16 or wider, within the bound.
A program may use at most 64 MiB of HBM per device.

```python
import math
import jax
import jax.numpy as jnp
import numpy as np
from jax import lax

NODE_DEV = 256
ITERS = 4
REACH = 4
PIPES_DEV = 512
IFACE_C = 64
CAPH = 128
NODES = 32768
PIPES = 65536
SAMPLES = 256
LOAD_ROWS = 16384
N_DOM = 128


def draw_pipe_ends(key, part):
    first_key, second_key = jax.random.split(jax.random.fold_in(key, 11))
    start = jax.random.randint(first_key, (PIPES,), 0, NODE_DEV)
    offset = jax.random.randint(second_key, (PIPES,), 1, NODE_DEV)
    return jnp.stack([start, (start + offset) % NODE_DEV]).astype(jnp.int32)


def set_ends(entries, rng, low, high):
    index_at = [jax.random.randint(jax.random.fold_in(rng, axis), (), 0, length) for axis, length in enumerate(entries.shape)]
    widest = entries.shape.index(max(entries.shape))
    next_to = index_at[:widest] + [(index_at[widest] + 1) % entries.shape[widest]] + index_at[widest + 1:]
    return entries.at[tuple(index_at)].set(low).at[tuple(next_to)].set(high)


def block_levels(rng, shape, shards, smallest, top_value):
    def one(position, blocks):
        steps = jax.random.uniform(jax.random.fold_in(jax.random.fold_in(rng, 6), position), (blocks,), jnp.float32, smallest / len(shards), top_value / len(shards))
        return jnp.repeat(jnp.exp(steps), shape[position] // blocks).reshape((-1,) + (1,) * (len(shape) - position - 1))

    gain = one(*shards[0])
    for cut in shards[1:]:
        gain = gain * one(*cut)
    return gain


def profile(amount, total, limit, skew):
    weights = [(1 << 20) // math.isqrt(standing ** skew) + 1 for standing in range(2, amount + 1)]
    rest, holding = total - limit - (amount - 1), [1] * (amount - 1)
    while rest > 0:
        movable = [i for i in range(amount - 1) if holding[i] < limit]
        pool, left = sum([weights[i] for i in movable]), rest
        for i in movable:
            extra = min(limit - holding[i], max(1, left * weights[i] // pool), rest)
            holding[i] = holding[i] + extra
            rest = rest - extra
    return np.array([limit] + holding)


def uneven_parts(own_key, number_of, total, bound, lean):
    if number_of == 2:
        one = jax.random.randint(own_key, (), max(1, total - bound), min(bound, total - 1) + 1)
        return jnp.stack([one, total - one])
    lengths = jnp.asarray(profile(number_of, total, bound, lean), jnp.int32)
    twos = (number_of - 1) // 2
    source_of, sink = lengths[1:1 + 2 * twos:2], lengths[2:2 + 2 * twos:2]
    margin = jnp.minimum(source_of - 1, bound - sink)
    moved = jax.random.randint(jax.random.fold_in(own_key, 1), (twos,), 0, 1 << 20) % (margin + 1)
    lengths = lengths.at[1:1 + 2 * twos:2].set(source_of - moved).at[2:2 + 2 * twos:2].set(sink + moved)
    return lengths[jax.random.permutation(jax.random.fold_in(own_key, 2), number_of)]


def normal_values(own_key, extent, scale, most, cuts=(), kind=jnp.bfloat16):
    array = jax.random.normal(own_key, extent, jnp.float32) * scale
    if len(cuts) > 0:
        array = block_levels(own_key, extent, cuts, -0.22, 0.18) * array
    return jnp.clip(array, min=-most, max=most).astype(kind)


def setup_inputs(seed: int = 0) -> dict:
    streams_of = jax.random.split(jax.random.key(seed), 10)
    return {
        "state": normal_values(streams_of[0], (2, NODES, SAMPLES), 1.0, 6.0, ((1, 128), (2, 2)), jnp.float32),
        "demand_load": jnp.clip(jnp.exp(math.log(2.0) - 2.9996462 * jax.random.uniform(streams_of[1], (2, SAMPLES, LOAD_ROWS), jnp.float32) ** block_levels(streams_of[1], (2, SAMPLES, LOAD_ROWS), ((0, 2), (1, 128)), -0.2, 0.2)), 0.099609375, 2.0).astype(jnp.bfloat16),
        "node_coef": jnp.clip(jnp.exp(math.log(2.0) - 2.3025851 * jax.random.uniform(streams_of[2], (2, NODES), jnp.float32) ** block_levels(streams_of[2], (2, NODES), ((1, 128),), -0.2, 0.2)), 0.2, 2.0),
        "pipe_ends": draw_pipe_ends(jax.random.fold_in(streams_of[9], 71), 0),
        "pipe_coef": jnp.clip(jnp.exp(math.log(2.0) - 1.3862944 * jax.random.uniform(streams_of[4], (2, PIPES), jnp.float32) ** block_levels(streams_of[4], (2, PIPES), ((1, 128),), -0.2, 0.2)), 0.5, 2.0),
        "iface_node": set_ends(jax.random.randint(streams_of[5], (N_DOM, 4, IFACE_C), 0, NODE_DEV), jax.random.fold_in(streams_of[5], 1), 0, NODE_DEV - 1).astype(jnp.int32),
        "iface_coef": jnp.clip(jnp.exp(jax.random.uniform(streams_of[6], (2, N_DOM, 2, IFACE_C), jnp.float32, math.log(0.5), math.log(2.0))), 0.5, 2.0),
        "cons_node": set_ends(jax.random.randint(streams_of[7], (N_DOM, 2 * CAPH), 0, NODE_DEV), jax.random.fold_in(streams_of[7], 1), 0, NODE_DEV - 1).astype(jnp.int32),
        "cons_count": uneven_parts(streams_of[8], N_DOM, N_DOM * CAPH, 2 * CAPH, 2).astype(jnp.int32),
    }


def pipe_flux(head_from, head_to, temp_from, temp_to, conduct, spread):
    drop = head_from - head_to
    flow = conduct * drop * lax.rsqrt(jnp.sqrt(1.0 + drop * drop))
    mixing = 0.5 * jnp.sqrt(flow * flow + spread * spread)
    heat = 0.5 * flow * (temp_from + temp_to) + mixing * (temp_from - temp_to)
    return (flow, heat)

def pipe_slopes(head_from, head_to, temp_from, temp_to, conduct, spread):
    drop = head_from - head_to
    square = 1.0 + drop * drop
    quarter = lax.rsqrt(jnp.sqrt(square))
    flow = conduct * drop * quarter
    slope = conduct * (1.0 + 0.5 * drop * drop) / square * quarter
    mixing = 0.5 * jnp.sqrt(flow * flow + spread * spread)
    heat_slope = 0.5 * (temp_from + temp_to) + (temp_from - temp_to) * flow / (4.0 * mixing)
    return (slope, heat_slope, 0.5 * flow + mixing, 0.5 * flow - mixing)

def reference(state, demand_load, node_coef, pipe_ends, pipe_coef, iface_node, iface_coef, cons_node, cons_count):
    parts = jnp.arange(N_DOM, dtype=jnp.int32)
    offsets = (1, -1, REACH, -REACH)
    partner_colour = (1, 0, 3, 2)
    owner = jnp.arange(PIPES, dtype=jnp.int32) // PIPES_DEV * NODE_DEV
    from_ids = pipe_ends[0] + owner
    to_ids = pipe_ends[1] + owner
    near_list = []
    far_list = []
    coef_list = []
    for colour in range(4):
        partner = (parts + offsets[colour]) % N_DOM
        near_list.append((iface_node[:, colour, :] + parts[:, None] * NODE_DEV).reshape(-1))
        far_list.append((iface_node[partner, partner_colour[colour], :] + partner[:, None] * NODE_DEV).reshape(-1))
        if offsets[colour] > 0:
            coef = iface_coef[:, :, colour // 2, :]
        else:
            coef = iface_coef[:, partner, partner_colour[colour] // 2, :]
        coef_list.append(coef.reshape(2, -1))
    near_ids = jnp.concatenate(near_list)
    far_ids = jnp.concatenate(far_list)
    icoef = jnp.concatenate(coef_list, axis=1)
    start_ids = jnp.concatenate([from_ids, near_ids])
    end_ids = jnp.concatenate([to_ids, far_ids])
    target_ids = jnp.concatenate([from_ids, near_ids, to_ids])
    conduct = jnp.concatenate([pipe_coef[0], icoef[0]])[:, None]
    spread = jnp.concatenate([pipe_coef[1], icoef[1]])[:, None]
    inner = PIPES
    demand = demand_load.reshape(2, SAMPLES, N_DOM, CAPH).transpose(2, 0, 3, 1).reshape(N_DOM, 2 * CAPH, SAMPLES)
    demand = demand.astype(jnp.float32)
    live = jnp.arange(2 * CAPH, dtype=jnp.int32)[None, :] < cons_count[:, None]
    demand = jnp.where(live[:, :, None], demand, jnp.float32(0.0))
    cons_ids = (cons_node + parts[:, None] * NODE_DEV).reshape(-1)
    usage_all = jnp.zeros((NODES, SAMPLES), jnp.float32).at[cons_ids].add(demand.reshape(-1, SAMPLES))
    width = math.gcd(SAMPLES, 32)
    blocks = SAMPLES // width
    fields = state.reshape(2, NODES, blocks, width).transpose(2, 0, 1, 3)
    usages = usage_all.reshape(NODES, blocks, width).transpose(1, 0, 2)

    def solve(args):
        field, usage = args
        storage = node_coef[0][:, None]
        cooling = node_coef[1][:, None] + usage

        def balance(values):
            head, temp = (values[0], values[1])
            flow, heat = pipe_flux(head[start_ids], head[end_ids], temp[start_ids], temp[end_ids], conduct, spread)
            moved = jnp.stack([flow, heat])
            moved = jnp.concatenate([moved, -moved[:, :inner]], axis=1)
            net = jnp.zeros((2, NODES, width), jnp.float32).at[:, target_ids].add(moved)
            return net + jnp.stack([storage * head + usage, cooling * temp])
        resid = balance(field)
        head, temp = (field[0], field[1])
        slope, heat_slope, upper, lower = pipe_slopes(head[start_ids], head[end_ids], temp[start_ids], temp[end_ids], conduct, spread)
        blank = jnp.zeros((NODES, width), jnp.float32)
        diag_head = storage + blank.at[target_ids].add(jnp.concatenate([slope, slope[:inner]]))
        diag_temp = cooling + blank.at[target_ids].add(jnp.concatenate([upper, -lower[:inner]]))
        mixed = heat_slope * slope
        cross = blank.at[target_ids].add(jnp.concatenate([mixed, mixed[:inner]]))

        def precond(vec):
            first = vec[0] / diag_head
            return jnp.stack([first, (vec[1] - cross * first) / diag_temp])
        step = -precond(resid)
        for turn in range(ITERS):
            image = jax.jvp(balance, (field,), (step,))[1]
            step = step - precond(resid + image)
        return jnp.stack([step, resid])
    result = lax.map(solve, (fields, usages))
    result = result.transpose(1, 2, 3, 0, 4).reshape(2, 2, NODES, SAMPLES)
    return (result[0], result[1])
```

```python
import jax
import jax.numpy as jnp
from jax import lax
from jax.experimental import pallas as pl
from jax.experimental.pallas import tpu as pltpu
from jax.sharding import PartitionSpec as P

ITERS = 4
REACH = 4
MESH = pl.DeviceIdType.MESH
F32 = jnp.float32
BF16 = jnp.bfloat16

NODES = 256
PIPES = 512
IFACE = 64
FACES = 4 * IFACE
WIDTH = 128
SLOTS = 128
N_DOM = 128
HALF_DOM = N_DOM // 2
PARTNER_COLOUR = (1, 0, 3, 2)


def split(value):
    high = value.astype(BF16)
    return high, (value - high.astype(F32)).astype(BF16)


def mm(table, value):
    return jnp.dot(table, value, preferred_element_type=F32)


def column(row):
    return jnp.transpose(jnp.broadcast_to(row, (WIDTH, row.shape[1])))


def two(left, right):
    return jnp.concatenate([left, right], axis=1)


def onehot(condition):
    return jnp.where(condition, F32(1.0), F32(0.0))


def pipe_terms(drop, temp_sum, temp_drop, conduct, spread):
    square = 1.0 + drop * drop
    half_power = lax.rsqrt(square)
    quarter = jnp.sqrt(half_power)
    flow = conduct * drop * quarter
    slope = conduct * (1.0 + 0.5 * drop * drop) * half_power * half_power * quarter
    under = flow * flow + spread * spread
    inverse = lax.rsqrt(under)
    half_flow = 0.5 * flow
    mixing = 0.5 * under * inverse
    heat = half_flow * temp_sum + mixing * temp_drop
    heat_slope = 0.5 * temp_sum + temp_drop * half_flow * inverse
    return flow, heat, slope, heat_slope * slope, half_flow, mixing


def kernel(
    state_hbm,
    demand_hbm,
    node_coef_hbm,
    pipe_ends_hbm,
    pipe_coef_hbm,
    iface_node_hbm,
    iface_coef_hbm,
    cons_node_hbm,
    cons_count_hbm,
    step_hbm,
    resid_hbm,
    state,
    demand,
    node_coef,
    pipe_ends,
    pipe_coef,
    iface_node,
    iface_coef,
    cons_node,
    cons_count,
    rows_in,
    rows,
    faces_out,
    faces_in,
    m_nodes,
    a_nodes,
    m_pipes,
    a_pipes,
    f_nodes,
    f_faces,
    inner,
    outer,
    node,
    serves,
    high,
    low,
    pipe_high,
    pipe_low,
    face_high,
    face_low,
    extra_high,
    extra_low,
    mixed_both,
    rho,
    delta,
    step,
    resid,
    load_sem,
    out_sem,
    rows_send,
    rows_self_send,
    rows_recv,
    face_send,
    face_recv,
):
    rank = lax.axis_index("dom")
    core = lax.axis_index("samp")
    owner_half = rank // HALF_DOM
    left = slice(0, WIDTH)
    right = slice(WIDTH, 2 * WIDTH)

    barrier = pltpu.get_barrier_semaphore()
    around = [lax.rem(rank + o + N_DOM, N_DOM) for o in (1, -1, REACH, -REACH)]
    for j in range(HALF_DOM):
        for c in range(2):
            pl.semaphore_signal(
                barrier,
                inc=1,
                device_id=(HALF_DOM * core + lax.rem(rank + j, HALF_DOM), c),
                device_id_type=MESH,
            )
    for q in around:
        pl.semaphore_signal(barrier, inc=1, device_id=(q, core), device_id_type=MESH)

    loads = [
        (iface_node_hbm, iface_node),
        (state_hbm, state),
        (demand_hbm, demand),
        (node_coef_hbm, node_coef),
        (pipe_ends_hbm, pipe_ends),
        (pipe_coef_hbm, pipe_coef),
        (cons_node_hbm, cons_node),
        (cons_count_hbm, cons_count),
        (iface_coef_hbm, iface_coef),
    ]
    loads = [
        pltpu.make_async_copy(src, dst, load_sem.at[i]) for i, (src, dst) in enumerate(loads)
    ]
    for load in loads:
        load.start()

    def chunk(i, size):
        return slice(i * size, (i + 1) * size)

    loads[0].wait()
    face_rows = [iface_node[0, c : c + 1, :].astype(F32) for c in range(4)]
    lane_of_node = lax.broadcasted_iota(jnp.int32, (IFACE, WIDTH), 1).astype(F32)
    for c in range(4):
        ids = column(face_rows[c])
        for part in range(NODES // WIDTH):
            f_faces[chunk(c, IFACE), chunk(part, WIDTH)] = onehot(
                ids == lane_of_node + float(part * WIDTH)
            ).astype(BF16)
    loads[1].wait()
    for i in range(2):
        for f in range(2):
            high[chunk(i, 128), chunk(f, WIDTH)], low[chunk(i, 128), chunk(f, WIDTH)] = split(
                state[f, chunk(i, 128), :]
            )

    def face_copies(turn):
        return [
            pltpu.make_async_remote_copy(
                src_ref=faces_out.at[turn, c],
                dst_ref=faces_in.at[turn, PARTNER_COLOUR[c]],
                send_sem=face_send.at[turn, c],
                recv_sem=face_recv.at[turn, PARTNER_COLOUR[c]],
                device_id=(around[c], core),
                device_id_type=MESH,
            )
            for c in range(4)
        ]

    def face_values(turn, c):
        table = f_faces[chunk(c, IFACE), :]
        faces_out[turn, c] = mm(table, high[...]) + mm(table, low[...])

    def pipe_drops(i):
        at = chunk(i, 128)
        drops = mm(m_pipes[at, :], high[...]) + mm(m_pipes[at, :], low[...])
        sums = mm(a_pipes[at, :], two(high[:, right], low[:, right]))
        return drops[:, left], drops[:, right], sums[:, left] + sums[:, right]

    copies = face_copies(0)
    for c in range(4):
        face_values(0, c)
    loads[2].wait()
    pl.semaphore_wait(barrier, N_DOM + 4)
    for copy in copies:
        copy.start()

    slot = core * HALF_DOM + lax.rem(rank, HALF_DOM)
    for k in range(1, N_DOM):
        p = lax.rem(rank + k, N_DOM)
        pltpu.make_async_remote_copy(
            src_ref=demand.at[0, :, pl.ds(pl.multiple_of(p * SLOTS, SLOTS), SLOTS)],
            dst_ref=rows_in.at[slot],
            send_sem=rows_send,
            recv_sem=rows_recv,
            device_id=(p, owner_half),
            device_id_type=MESH,
        ).start()
    own_rows = demand.at[0, :, pl.ds(pl.multiple_of(rank * SLOTS, SLOTS), SLOTS)]

    @pl.when(owner_half == core)
    def _():
        pltpu.make_async_copy(own_rows, rows_in.at[slot], rows_recv).start()

    across = pltpu.make_async_remote_copy(
        src_ref=own_rows,
        dst_ref=rows_in.at[slot],
        send_sem=rows_self_send,
        recv_sem=rows_recv,
        device_id=(rank, 1 - core),
        device_id_type=MESH,
    )

    @pl.when(owner_half != core)
    def _():
        across.start()

    for load in loads[3:]:
        load.wait()

    for i in range(NODES // 128):
        node_of_row = lax.broadcasted_iota(jnp.int32, (128, PIPES), 0) + i * 128
        at_start = onehot(pipe_ends[0:1, :] == node_of_row)
        at_end = onehot(pipe_ends[1:2, :] == node_of_row)
        m_nodes[chunk(i, 128), :] = (at_start - at_end).astype(BF16)
        a_nodes[chunk(i, 128), :] = (at_start + at_end).astype(BF16)
    lane_of_node = lax.broadcasted_iota(jnp.int32, (128, WIDTH), 1).astype(F32)
    for i in range(PIPES // 128):
        start_ids = column(pipe_ends[0:1, chunk(i, 128)].astype(F32))
        end_ids = column(pipe_ends[1:2, chunk(i, 128)].astype(F32))
        for part in range(NODES // WIDTH):
            at_start = onehot(start_ids == lane_of_node + float(part * WIDTH))
            at_end = onehot(end_ids == lane_of_node + float(part * WIDTH))
            m_pipes[chunk(i, 128), chunk(part, WIDTH)] = (at_start - at_end).astype(BF16)
            a_pipes[chunk(i, 128), chunk(part, WIDTH)] = (at_start + at_end).astype(BF16)
    face_ids = jnp.concatenate(face_rows, axis=1)
    for i in range(NODES // 128):
        node_of_row = lax.broadcasted_iota(jnp.int32, (128, FACES), 0) + i * 128
        f_nodes[chunk(i, 128), :] = onehot(face_ids == node_of_row.astype(F32)).astype(BF16)

    def scatter(table, i, upper, lower):
        return mm(table[chunk(i, 128), :], upper[...]) + mm(table[chunk(i, 128), :], lower[...])

    for i in range(PIPES // 128):
        at = chunk(i, 128)
        drop, temp_drop, temp_sum = pipe_drops(i)
        flow, heat, slope, mixed, half_flow, mixing = pipe_terms(
            drop, temp_sum, temp_drop, column(pipe_coef[0:1, at]), column(pipe_coef[1:2, at])
        )
        inner[0, at], inner[1, at], inner[2, at], inner[3, at] = slope, mixed, half_flow, mixing
        pipe_high[at, left], pipe_low[at, left] = split(flow)
        pipe_high[at, right], pipe_low[at, right] = split(heat)
        extra_high[at, left], extra_low[at, left] = split(slope)
        extra_high[at, right], extra_low[at, right] = split(mixing)
        mixed_both[at, left], mixed_both[at, right] = split(mixed)
    for i in range(NODES // 128):
        at = chunk(i, 128)
        rho[at, :] = scatter(m_nodes, i, pipe_high, pipe_low)
        slopes = scatter(a_nodes, i, extra_high, extra_low)
        cross = mm(a_nodes[at, :], mixed_both[...])
        node[0, at] = column(node_coef[0:1, at])
        node[1, at] = column(node_coef[1:2, at])
        node[2, at] = node[0, at] + slopes[:, left]
        node[3, at] = 0.5 * rho[at, left] + slopes[:, right]
        node[4, at] = cross[:, left] + cross[:, right]
        live = lax.broadcasted_iota(jnp.int32, (128, 2 * SLOTS), 1) < cons_count[...]
        here = cons_node[...] == lax.broadcasted_iota(jnp.int32, (128, 2 * SLOTS), 0) + i * 128
        serves[at, :] = onehot(jnp.logical_and(live, here)).astype(BF16)

    step[...] = jnp.zeros_like(step)

    lane = lax.broadcasted_iota(jnp.int32, (IFACE, N_DOM), 1)

    def iface_column(which, c):
        owner = (rank, around[1], rank, around[3])[c]
        mine = jnp.where(lane == owner, iface_coef[which, c // 2], F32(0.0))
        return jnp.broadcast_to(jnp.sum(mine, axis=1, keepdims=True), (IFACE, WIDTH))

    for c in range(4):
        outer[0, chunk(c, IFACE)] = iface_column(0, c)
        outer[1, chunk(c, IFACE)] = iface_column(1, c)
    for copy in copies:
        copy.wait_recv()
    for c in range(4):
        at = chunk(c, IFACE)
        near_head, near_temp = faces_out[0, c, :, left], faces_out[0, c, :, right]
        far_head, far_temp = faces_in[0, c, :, left], faces_in[0, c, :, right]
        flow, heat, slope, mixed, half_flow, mixing = pipe_terms(
            near_head - far_head, near_temp + far_temp, near_temp - far_temp, outer[0, at], outer[1, at]
        )
        upper = half_flow + mixing
        outer[0, at], outer[1, at], outer[2, at], outer[3, at] = slope, mixed, upper, half_flow - mixing
        face_high[at, left], face_low[at, left] = split(flow)
        face_high[at, right], face_low[at, right] = split(heat)
        extra_high[at, left], extra_low[at, left] = split(slope)
        extra_high[at, right], extra_low[at, right] = split(upper)
        mixed_both[at, left], mixed_both[at, right] = split(mixed)
    for i in range(NODES // 128):
        at = chunk(i, 128)
        rho[at, :] += scatter(f_nodes, i, face_high, face_low)
        table = f_nodes[at, :]
        slopes = mm(table, extra_high[:FACES, :]) + mm(table, extra_low[:FACES, :])
        cross = mm(table, mixed_both[:FACES, :])
        node[2, at] = 1.0 / (node[2, at] + slopes[:, left])
        node[3, at] += slopes[:, right]
        node[4, at] += cross[:, left] + cross[:, right]

    def precondition(i):
        at = chunk(i, 128)
        head = -rho[at, left] * node[2, at]
        temp = -(rho[at, right] + node[4, at] * head) * node[3, at]
        delta[at, left] = head
        delta[at, right] = temp
        high[at, left], low[at, left] = split(head)
        high[at, right], low[at, right] = split(temp)

    pltpu.make_async_remote_copy(
        src_ref=rows_in,
        dst_ref=rows_in,
        send_sem=rows_send,
        recv_sem=rows_recv,
        device_id=(rank, 1 - core),
        device_id_type=MESH,
    ).wait_recv()
    for h in range(2):
        for j in range(HALF_DOM):
            rows[2 * j : 2 * j + 2, chunk(h, SLOTS)] = rows_in[h * HALF_DOM + j].astype(F32)
    for i in range(NODES // 128):
        at = chunk(i, 128)
        usage = lax.dot_general(
            serves[at, :],
            rows[...].astype(BF16),
            (((1,), (1,)), ((), ())),
            preferred_element_type=F32,
        )
        cooling = node[1, at] + usage
        node[1, at] = cooling
        node[3, at] = 1.0 / (node[3, at] + cooling)
        rho[at, left] += node[0, at] * state[0, at] + usage
        rho[at, right] += cooling * state[1, at]
        resid[0, at] = rho[at, left]
        resid[1, at] = rho[at, right]
        precondition(i)

    resid_out = pltpu.make_async_copy(resid, resid_hbm, out_sem.at[0])
    resid_out.start()

    def one_turn(turn, carry):
        copies = face_copies(turn)
        for c in range(4):
            face_values(turn, c)
            copies[c].start()
        for i in range(PIPES // 128):
            at = chunk(i, 128)
            drop, temp_drop, temp_sum = pipe_drops(i)
            pipe_high[at, left], pipe_low[at, left] = split(inner[0, at] * drop)
            pipe_high[at, right], pipe_low[at, right] = split(
                inner[1, at] * drop + inner[2, at] * temp_sum + inner[3, at] * temp_drop
            )
        for c in range(4):
            at = chunk(c, IFACE)
            head, temp = faces_out[turn, c, :, left], faces_out[turn, c, :, right]
            face_high[at, left], face_low[at, left] = split(outer[0, at] * head)
            face_high[at, right], face_low[at, right] = split(outer[1, at] * head + outer[2, at] * temp)
        for i in range(NODES // 128):
            at = chunk(i, 128)
            moved = scatter(m_nodes, i, pipe_high, pipe_low) + scatter(f_nodes, i, face_high, face_low)
            head, temp = delta[at, left], delta[at, right]
            rho[at, left] += moved[:, left] + node[0, at] * head
            rho[at, right] += moved[:, right] + node[1, at] * temp
            step[0, at] += head
            step[1, at] += temp
        for copy in copies:
            copy.wait_recv()
        for c in range(4):
            at = chunk(c, IFACE)
            head, temp = faces_in[turn, c, :, left], faces_in[turn, c, :, right]
            face_high[at, left], face_low[at, left] = split(-outer[0, at] * head)
            face_high[at, right], face_low[at, right] = split(outer[3, at] * temp - outer[1, at] * head)
        for i in range(NODES // 128):
            at = chunk(i, 128)
            rho[at, :] += scatter(f_nodes, i, face_high, face_low)
            precondition(i)
        return carry

    lax.fori_loop(1, ITERS + 1, one_turn, 0)
    for i in range(NODES // 128):
        at = chunk(i, 128)
        step[0, at] += delta[at, left]
        step[1, at] += delta[at, right]
    step_out = pltpu.make_async_copy(step, step_hbm, out_sem.at[1])
    step_out.start()

    def sent(turn, carry):
        for copy in face_copies(turn):
            copy.wait_send()
        return carry

    lax.fori_loop(0, ITERS + 1, sent, 0)
    pltpu.make_async_remote_copy(
        src_ref=rows_in.at[pl.ds(0, N_DOM - 1)],
        dst_ref=rows_in.at[pl.ds(0, N_DOM - 1)],
        send_sem=rows_send,
        recv_sem=rows_recv,
        device_id=(rank, 1 - core),
        device_id_type=MESH,
    ).wait_send()

    @pl.when(owner_half != core)
    def _():
        across.wait_send()

    resid_out.wait()
    step_out.wait()


def shards(
    state,
    demand_load,
    node_coef,
    pipe_ends,
    pipe_coef,
    iface_node,
    iface_coef,
    cons_node,
    cons_count,
):
    vmem = pltpu.VMEM
    dma = pltpu.SemaphoreType.DMA
    anywhere = pl.BlockSpec(memory_space=pl.ANY)
    out = jax.ShapeDtypeStruct((2, NODES, WIDTH), F32)
    step, resid = pl.pallas_call(
        kernel,
        out_shape=(out, out),
        in_specs=[anywhere] * 9,
        out_specs=(anywhere, anywhere),
        scratch_shapes=[
            vmem((2, NODES, WIDTH), F32),
            vmem((1, 2, N_DOM * SLOTS), BF16),
            vmem((2, NODES), F32),
            vmem((2, PIPES), jnp.int32),
            vmem((2, PIPES), F32),
            vmem((1, 4, IFACE), jnp.int32),
            vmem((2, 2, IFACE, N_DOM), F32),
            vmem((1, 2 * SLOTS), jnp.int32),
            vmem((1, 1), jnp.int32),
            vmem((N_DOM, 2, SLOTS), BF16),
            vmem((WIDTH, 2 * SLOTS), F32),
            vmem((ITERS + 1, 4, IFACE, 2 * WIDTH), F32),
            vmem((ITERS + 1, 4, IFACE, 2 * WIDTH), F32),
            vmem((NODES, PIPES), BF16),
            vmem((NODES, PIPES), BF16),
            vmem((PIPES, NODES), BF16),
            vmem((PIPES, NODES), BF16),
            vmem((NODES, FACES), BF16),
            vmem((FACES, NODES), BF16),
            vmem((4, PIPES, WIDTH), F32),
            vmem((4, FACES, WIDTH), F32),
            vmem((5, NODES, WIDTH), F32),
            vmem((NODES, 2 * SLOTS), BF16),
            vmem((NODES, 2 * WIDTH), BF16),
            vmem((NODES, 2 * WIDTH), BF16),
            vmem((PIPES, 2 * WIDTH), BF16),
            vmem((PIPES, 2 * WIDTH), BF16),
            vmem((FACES, 2 * WIDTH), BF16),
            vmem((FACES, 2 * WIDTH), BF16),
            vmem((PIPES, 2 * WIDTH), BF16),
            vmem((PIPES, 2 * WIDTH), BF16),
            vmem((PIPES, 2 * WIDTH), BF16),
            vmem((NODES, 2 * WIDTH), F32),
            vmem((NODES, 2 * WIDTH), F32),
            vmem((2, NODES, WIDTH), F32),
            vmem((2, NODES, WIDTH), F32),
            dma((9,)),
            dma((2,)),
            dma,
            dma,
            dma,
            dma((ITERS + 1, 4)),
            dma((ITERS + 1, 4)),
        ],
        compiler_params=pltpu.CompilerParams(
            collective_id=0, has_side_effects=True, vmem_limit_bytes=56 << 20
        ),
        name="newton_step",
    )(
        state,
        demand_load,
        node_coef,
        pipe_ends,
        pipe_coef,
        iface_node,
        jnp.transpose(iface_coef, (0, 2, 3, 1)),
        cons_node,
        cons_count.reshape(1, 1),
    )
    return step, resid


def solution(mesh):
    placed = (
        P(None, "dom", "samp"),
        P("samp", "dom", None),
        P(None, "dom"),
        P(None, "dom"),
        P(None, "dom"),
        P("dom", None, None),
        P(),
        P("dom", None),
        P("dom"),
    )
    return jax.shard_map(
        shards,
        mesh=mesh,
        in_specs=placed,
        out_specs=(P(None, "dom", "samp"), P(None, "dom", "samp")),
        check_vma=False,
    )
```

```python
import jax
import jax.numpy as jnp
from jax import lax
from jax.experimental import pallas as pl
from jax.experimental.pallas import tpu as pltpu
from jax.sharding import PartitionSpec as P

ITERS = 4
REACH = 4
MESH = pl.DeviceIdType.MESH
F32 = jnp.float32
BF16 = jnp.bfloat16

NODES = 256
PIPES = 512
IFACE = 64
FACES = 4 * IFACE
WIDTH = 128
SLOTS = 128
N_DOM = 128
HALF_DOM = N_DOM // 2
PARTNER_COLOUR = (1, 0, 3, 2)
DEEP = 8
FAR_FIRST_Z = (4, 3, 5, 2, 6, 1, 7, 0)
FAR_FIRST_X = (2, 1, 3, 0)


def split(value):
    high = value.astype(BF16)
    return high, (value - high.astype(F32)).astype(BF16)


def mm(table, value):
    return jnp.dot(table, value, preferred_element_type=F32)


def column(row):
    return jnp.transpose(jnp.broadcast_to(row, (WIDTH, row.shape[1])))


def two(left, right):
    return jnp.concatenate([left, right], axis=1)


def onehot(condition):
    return jnp.where(condition, F32(1.0), F32(0.0))


def pipe_terms(drop, temp_sum, temp_drop, conduct, spread):
    square = 1.0 + drop * drop
    half_power = lax.rsqrt(square)
    quarter = jnp.sqrt(half_power)
    flow = conduct * drop * quarter
    slope = conduct * (1.0 + 0.5 * drop * drop) * half_power * half_power * quarter
    under = flow * flow + spread * spread
    inverse = lax.rsqrt(under)
    half_flow = 0.5 * flow
    mixing = 0.5 * under * inverse
    heat = half_flow * temp_sum + mixing * temp_drop
    heat_slope = 0.5 * temp_sum + temp_drop * half_flow * inverse
    return flow, heat, slope, heat_slope * slope, half_flow, mixing


def kernel(
    state_hbm,
    demand_hbm,
    node_coef_hbm,
    pipe_ends_hbm,
    pipe_coef_hbm,
    iface_node_hbm,
    iface_coef_hbm,
    cons_node_hbm,
    cons_count_hbm,
    step_hbm,
    resid_hbm,
    state,
    demand,
    node_coef,
    pipe_ends,
    pipe_coef,
    iface_node,
    iface_coef,
    cons_node,
    cons_count,
    relay,
    rows_in,
    rows,
    faces_out,
    faces_in,
    m_nodes,
    a_nodes,
    m_pipes,
    a_pipes,
    f_nodes,
    f_faces,
    inner,
    outer,
    node,
    serves,
    high,
    low,
    pipe_high,
    pipe_low,
    face_high,
    face_low,
    extra_high,
    extra_low,
    mixed_both,
    rho,
    delta,
    step,
    resid,
    load_sem,
    out_sem,
    relay_send,
    relay_recv,
    rows_send,
    rows_self_send,
    rows_recv,
    face_send,
    face_recv,
):
    rank = lax.axis_index("dom")
    core = lax.axis_index("samp")
    owner_half = rank // HALF_DOM
    left = slice(0, WIDTH)
    right = slice(WIDTH, 2 * WIDTH)

    at_y, at_z, at_x = rank // 32, lax.rem(rank // REACH, DEEP), lax.rem(rank, REACH)

    def place(y, z, x):
        return 32 * y + REACH * z + x

    barrier = pltpu.get_barrier_semaphore()
    around = [lax.rem(rank + o + N_DOM, N_DOM) for o in (1, -1, REACH, -REACH)]
    for dz in FAR_FIRST_Z[:-1]:
        pl.semaphore_signal(
            barrier,
            inc=1,
            device_id=(place(at_y, lax.rem(at_z + dz, DEEP), at_x), core),
            device_id_type=MESH,
        )
    for dx in FAR_FIRST_X:
        for y in range(2):
            for c in range(2):
                source = place(2 * core + y, at_z, lax.rem(at_x + dx, REACH))
                pl.semaphore_signal(barrier, inc=1, device_id=(source, c), device_id_type=MESH)
    for q in around:
        pl.semaphore_signal(barrier, inc=1, device_id=(q, core), device_id_type=MESH)

    loads = [
        (iface_node_hbm, iface_node),
        (state_hbm, state),
        (demand_hbm, demand),
        (node_coef_hbm, node_coef),
        (pipe_ends_hbm, pipe_ends),
        (pipe_coef_hbm, pipe_coef),
        (cons_node_hbm, cons_node),
        (cons_count_hbm, cons_count),
        (iface_coef_hbm, iface_coef),
    ]
    loads = [
        pltpu.make_async_copy(src, dst, load_sem.at[i]) for i, (src, dst) in enumerate(loads)
    ]
    for load in loads:
        load.start()

    def chunk(i, size):
        return slice(i * size, (i + 1) * size)

    loads[0].wait()
    face_rows = [iface_node[0, c : c + 1, :].astype(F32) for c in range(4)]
    lane_of_node = lax.broadcasted_iota(jnp.int32, (IFACE, WIDTH), 1).astype(F32)
    for c in range(4):
        ids = column(face_rows[c])
        for part in range(NODES // WIDTH):
            f_faces[chunk(c, IFACE), chunk(part, WIDTH)] = onehot(
                ids == lane_of_node + float(part * WIDTH)
            ).astype(BF16)
    loads[1].wait()
    for i in range(2):
        for f in range(2):
            high[chunk(i, 128), chunk(f, WIDTH)], low[chunk(i, 128), chunk(f, WIDTH)] = split(
                state[f, chunk(i, 128), :]
            )

    def face_copies(turn):
        return [
            pltpu.make_async_remote_copy(
                src_ref=faces_out.at[turn, c],
                dst_ref=faces_in.at[turn, PARTNER_COLOUR[c]],
                send_sem=face_send.at[turn, c],
                recv_sem=face_recv.at[turn, PARTNER_COLOUR[c]],
                device_id=(around[c], core),
                device_id_type=MESH,
            )
            for c in range(4)
        ]

    def face_values(turn, c):
        table = f_faces[chunk(c, IFACE), :]
        faces_out[turn, c] = mm(table, high[...]) + mm(table, low[...])

    def pipe_drops(i):
        at = chunk(i, 128)
        drops = mm(m_pipes[at, :], high[...]) + mm(m_pipes[at, :], low[...])
        sums = mm(a_pipes[at, :], two(high[:, right], low[:, right]))
        return drops[:, left], drops[:, right], sums[:, left] + sums[:, right]

    copies = face_copies(0)
    for c in range(4):
        face_values(0, c)
    loads[2].wait()
    pl.semaphore_wait(barrier, DEEP - 1 + 16 + 4)

    def rows_of(y, z):
        return demand.at[0, :, pl.ds(pl.multiple_of(place(y, z, 0) * SLOTS, SLOTS), REACH * SLOTS)]

    for dz in FAR_FIRST_Z[:-1]:
        z = lax.rem(at_z + dz, DEEP)
        for y in range(4):
            pltpu.make_async_remote_copy(
                src_ref=rows_of(y, z),
                dst_ref=relay.at[at_z, y],
                send_sem=relay_send,
                recv_sem=relay_recv,
                device_id=(place(at_y, z, at_x), core),
                device_id_type=MESH,
            ).start()
    for copy in copies:
        copy.start()
    for y in range(4):
        pltpu.make_async_copy(rows_of(y, at_z), relay.at[at_z, y], relay_recv).start()

    for load in loads[3:]:
        load.wait()

    for i in range(NODES // 128):
        node_of_row = lax.broadcasted_iota(jnp.int32, (128, PIPES), 0) + i * 128
        at_start = onehot(pipe_ends[0:1, :] == node_of_row)
        at_end = onehot(pipe_ends[1:2, :] == node_of_row)
        m_nodes[chunk(i, 128), :] = (at_start - at_end).astype(BF16)
        a_nodes[chunk(i, 128), :] = (at_start + at_end).astype(BF16)
    lane_of_node = lax.broadcasted_iota(jnp.int32, (128, WIDTH), 1).astype(F32)
    for i in range(PIPES // 128):
        start_ids = column(pipe_ends[0:1, chunk(i, 128)].astype(F32))
        end_ids = column(pipe_ends[1:2, chunk(i, 128)].astype(F32))
        for part in range(NODES // WIDTH):
            at_start = onehot(start_ids == lane_of_node + float(part * WIDTH))
            at_end = onehot(end_ids == lane_of_node + float(part * WIDTH))
            m_pipes[chunk(i, 128), chunk(part, WIDTH)] = (at_start - at_end).astype(BF16)
            a_pipes[chunk(i, 128), chunk(part, WIDTH)] = (at_start + at_end).astype(BF16)
    face_ids = jnp.concatenate(face_rows, axis=1)
    for i in range(NODES // 128):
        node_of_row = lax.broadcasted_iota(jnp.int32, (128, FACES), 0) + i * 128
        f_nodes[chunk(i, 128), :] = onehot(face_ids == node_of_row.astype(F32)).astype(BF16)

    def scatter(table, i, upper, lower):
        return mm(table[chunk(i, 128), :], upper[...]) + mm(table[chunk(i, 128), :], lower[...])

    for i in range(PIPES // 128):
        at = chunk(i, 128)
        drop, temp_drop, temp_sum = pipe_drops(i)
        flow, heat, slope, mixed, half_flow, mixing = pipe_terms(
            drop, temp_sum, temp_drop, column(pipe_coef[0:1, at]), column(pipe_coef[1:2, at])
        )
        inner[0, at], inner[1, at], inner[2, at], inner[3, at] = slope, mixed, half_flow, mixing
        pipe_high[at, left], pipe_low[at, left] = split(flow)
        pipe_high[at, right], pipe_low[at, right] = split(heat)
        extra_high[at, left], extra_low[at, left] = split(slope)
        extra_high[at, right], extra_low[at, right] = split(mixing)
        mixed_both[at, left], mixed_both[at, right] = split(mixed)
    for i in range(NODES // 128):
        at = chunk(i, 128)
        rho[at, :] = scatter(m_nodes, i, pipe_high, pipe_low)
        slopes = scatter(a_nodes, i, extra_high, extra_low)
        cross = mm(a_nodes[at, :], mixed_both[...])
        node[0, at] = column(node_coef[0:1, at])
        node[1, at] = column(node_coef[1:2, at])
        node[2, at] = node[0, at] + slopes[:, left]
        node[3, at] = 0.5 * rho[at, left] + slopes[:, right]
        node[4, at] = cross[:, left] + cross[:, right]
        live = lax.broadcasted_iota(jnp.int32, (128, 2 * SLOTS), 1) < cons_count[...]
        here = cons_node[...] == lax.broadcasted_iota(jnp.int32, (128, 2 * SLOTS), 0) + i * 128
        serves[at, :] = onehot(jnp.logical_and(live, here)).astype(BF16)

    step[...] = jnp.zeros_like(step)

    lane = lax.broadcasted_iota(jnp.int32, (IFACE, N_DOM), 1)

    def iface_column(which, c):
        owner = (rank, around[1], rank, around[3])[c]
        mine = jnp.where(lane == owner, iface_coef[which, c // 2], F32(0.0))
        return jnp.broadcast_to(jnp.sum(mine, axis=1, keepdims=True), (IFACE, WIDTH))

    for c in range(4):
        outer[0, chunk(c, IFACE)] = iface_column(0, c)
        outer[1, chunk(c, IFACE)] = iface_column(1, c)
    pltpu.make_async_remote_copy(
        src_ref=relay,
        dst_ref=relay,
        send_sem=relay_send,
        recv_sem=relay_recv,
        device_id=(rank, 1 - core),
        device_id_type=MESH,
    ).wait_recv()
    group = core * 8 + lax.rem(at_y, 2) * REACH + at_x

    def relayed(y, x):
        return relay.at[:, y, :, pl.ds(pl.multiple_of(x * SLOTS, SLOTS), SLOTS)]

    for dy in FAR_FIRST_X:
        for dx in FAR_FIRST_X:
            if (dy, dx) != (0, 0):
                y, x = lax.rem(at_y + dy, 4), lax.rem(at_x + dx, REACH)
                pltpu.make_async_remote_copy(
                    src_ref=relayed(y, x),
                    dst_ref=rows_in.at[group],
                    send_sem=rows_send,
                    recv_sem=rows_recv,
                    device_id=(place(y, at_z, x), owner_half),
                    device_id_type=MESH,
                ).start()
    own_rows = relayed(at_y, at_x)

    @pl.when(owner_half == core)
    def _():
        pltpu.make_async_copy(own_rows, rows_in.at[group], rows_recv).start()

    across = pltpu.make_async_remote_copy(
        src_ref=own_rows,
        dst_ref=rows_in.at[group],
        send_sem=rows_self_send,
        recv_sem=rows_recv,
        device_id=(rank, 1 - core),
        device_id_type=MESH,
    )

    @pl.when(owner_half != core)
    def _():
        across.start()

    for copy in copies:
        copy.wait_recv()
    for c in range(4):
        at = chunk(c, IFACE)
        near_head, near_temp = faces_out[0, c, :, left], faces_out[0, c, :, right]
        far_head, far_temp = faces_in[0, c, :, left], faces_in[0, c, :, right]
        flow, heat, slope, mixed, half_flow, mixing = pipe_terms(
            near_head - far_head, near_temp + far_temp, near_temp - far_temp, outer[0, at], outer[1, at]
        )
        upper = half_flow + mixing
        outer[0, at], outer[1, at], outer[2, at], outer[3, at] = slope, mixed, upper, half_flow - mixing
        face_high[at, left], face_low[at, left] = split(flow)
        face_high[at, right], face_low[at, right] = split(heat)
        extra_high[at, left], extra_low[at, left] = split(slope)
        extra_high[at, right], extra_low[at, right] = split(upper)
        mixed_both[at, left], mixed_both[at, right] = split(mixed)
    for i in range(NODES // 128):
        at = chunk(i, 128)
        rho[at, :] += scatter(f_nodes, i, face_high, face_low)
        table = f_nodes[at, :]
        slopes = mm(table, extra_high[:FACES, :]) + mm(table, extra_low[:FACES, :])
        cross = mm(table, mixed_both[:FACES, :])
        node[2, at] = 1.0 / (node[2, at] + slopes[:, left])
        node[3, at] += slopes[:, right]
        node[4, at] += cross[:, left] + cross[:, right]

    def precondition(i):
        at = chunk(i, 128)
        head = -rho[at, left] * node[2, at]
        temp = -(rho[at, right] + node[4, at] * head) * node[3, at]
        delta[at, left] = head
        delta[at, right] = temp
        high[at, left], low[at, left] = split(head)
        high[at, right], low[at, right] = split(temp)

    pltpu.make_async_remote_copy(
        src_ref=rows_in,
        dst_ref=rows_in,
        send_sem=rows_send,
        recv_sem=rows_recv,
        device_id=(rank, 1 - core),
        device_id_type=MESH,
    ).wait_recv()
    for h in range(2):
        for y in range(2):
            for z in range(DEEP):
                for x in range(REACH):
                    rows[chunk(place(y, z, x), 2), chunk(h, SLOTS)] = rows_in[
                        h * 8 + y * REACH + x, z
                    ].astype(F32)
    for i in range(NODES // 128):
        at = chunk(i, 128)
        usage = lax.dot_general(
            serves[at, :],
            rows[...].astype(BF16),
            (((1,), (1,)), ((), ())),
            preferred_element_type=F32,
        )
        cooling = node[1, at] + usage
        node[1, at] = cooling
        node[3, at] = 1.0 / (node[3, at] + cooling)
        rho[at, left] += node[0, at] * state[0, at] + usage
        rho[at, right] += cooling * state[1, at]
        resid[0, at] = rho[at, left]
        resid[1, at] = rho[at, right]
        precondition(i)

    resid_out = pltpu.make_async_copy(resid, resid_hbm, out_sem.at[0])
    resid_out.start()

    def one_turn(turn, carry):
        copies = face_copies(turn)
        for c in range(4):
            face_values(turn, c)
            copies[c].start()
        for i in range(PIPES // 128):
            at = chunk(i, 128)
            drop, temp_drop, temp_sum = pipe_drops(i)
            pipe_high[at, left], pipe_low[at, left] = split(inner[0, at] * drop)
            pipe_high[at, right], pipe_low[at, right] = split(
                inner[1, at] * drop + inner[2, at] * temp_sum + inner[3, at] * temp_drop
            )
        for c in range(4):
            at = chunk(c, IFACE)
            head, temp = faces_out[turn, c, :, left], faces_out[turn, c, :, right]
            face_high[at, left], face_low[at, left] = split(outer[0, at] * head)
            face_high[at, right], face_low[at, right] = split(outer[1, at] * head + outer[2, at] * temp)
        for i in range(NODES // 128):
            at = chunk(i, 128)
            moved = scatter(m_nodes, i, pipe_high, pipe_low) + scatter(f_nodes, i, face_high, face_low)
            head, temp = delta[at, left], delta[at, right]
            rho[at, left] += moved[:, left] + node[0, at] * head
            rho[at, right] += moved[:, right] + node[1, at] * temp
            step[0, at] += head
            step[1, at] += temp
        for copy in copies:
            copy.wait_recv()
        for c in range(4):
            at = chunk(c, IFACE)
            head, temp = faces_in[turn, c, :, left], faces_in[turn, c, :, right]
            face_high[at, left], face_low[at, left] = split(-outer[0, at] * head)
            face_high[at, right], face_low[at, right] = split(outer[3, at] * temp - outer[1, at] * head)
        for i in range(NODES // 128):
            at = chunk(i, 128)
            rho[at, :] += scatter(f_nodes, i, face_high, face_low)
            precondition(i)
        return carry

    lax.fori_loop(1, ITERS + 1, one_turn, 0)
    for i in range(NODES // 128):
        at = chunk(i, 128)
        step[0, at] += delta[at, left]
        step[1, at] += delta[at, right]
    step_out = pltpu.make_async_copy(step, step_hbm, out_sem.at[1])
    step_out.start()

    def sent(turn, carry):
        for copy in face_copies(turn):
            copy.wait_send()
        return carry

    lax.fori_loop(0, ITERS + 1, sent, 0)
    pltpu.make_async_remote_copy(
        src_ref=relay.at[pl.ds(0, DEEP - 1)],
        dst_ref=relay.at[pl.ds(0, DEEP - 1)],
        send_sem=relay_send,
        recv_sem=relay_recv,
        device_id=(rank, 1 - core),
        device_id_type=MESH,
    ).wait_send()
    pltpu.make_async_remote_copy(
        src_ref=rows_in.at[pl.ds(0, 15)],
        dst_ref=rows_in.at[pl.ds(0, 15)],
        send_sem=rows_send,
        recv_sem=rows_recv,
        device_id=(rank, 1 - core),
        device_id_type=MESH,
    ).wait_send()

    @pl.when(owner_half != core)
    def _():
        across.wait_send()

    resid_out.wait()
    step_out.wait()


def shards(
    state,
    demand_load,
    node_coef,
    pipe_ends,
    pipe_coef,
    iface_node,
    iface_coef,
    cons_node,
    cons_count,
):
    vmem = pltpu.VMEM
    dma = pltpu.SemaphoreType.DMA
    anywhere = pl.BlockSpec(memory_space=pl.ANY)
    out = jax.ShapeDtypeStruct((2, NODES, WIDTH), F32)
    step, resid = pl.pallas_call(
        kernel,
        out_shape=(out, out),
        in_specs=[anywhere] * 9,
        out_specs=(anywhere, anywhere),
        scratch_shapes=[
            vmem((2, NODES, WIDTH), F32),
            vmem((1, 2, N_DOM * SLOTS), BF16),
            vmem((2, NODES), F32),
            vmem((2, PIPES), jnp.int32),
            vmem((2, PIPES), F32),
            vmem((1, 4, IFACE), jnp.int32),
            vmem((2, 2, IFACE, N_DOM), F32),
            vmem((1, 2 * SLOTS), jnp.int32),
            vmem((1, 1), jnp.int32),
            vmem((DEEP, 4, 2, REACH * SLOTS), BF16),
            vmem((16, DEEP, 2, SLOTS), BF16),
            vmem((WIDTH, 2 * SLOTS), F32),
            vmem((ITERS + 1, 4, IFACE, 2 * WIDTH), F32),
            vmem((ITERS + 1, 4, IFACE, 2 * WIDTH), F32),
            vmem((NODES, PIPES), BF16),
            vmem((NODES, PIPES), BF16),
            vmem((PIPES, NODES), BF16),
            vmem((PIPES, NODES), BF16),
            vmem((NODES, FACES), BF16),
            vmem((FACES, NODES), BF16),
            vmem((4, PIPES, WIDTH), F32),
            vmem((4, FACES, WIDTH), F32),
            vmem((5, NODES, WIDTH), F32),
            vmem((NODES, 2 * SLOTS), BF16),
            vmem((NODES, 2 * WIDTH), BF16),
            vmem((NODES, 2 * WIDTH), BF16),
            vmem((PIPES, 2 * WIDTH), BF16),
            vmem((PIPES, 2 * WIDTH), BF16),
            vmem((FACES, 2 * WIDTH), BF16),
            vmem((FACES, 2 * WIDTH), BF16),
            vmem((PIPES, 2 * WIDTH), BF16),
            vmem((PIPES, 2 * WIDTH), BF16),
            vmem((PIPES, 2 * WIDTH), BF16),
            vmem((NODES, 2 * WIDTH), F32),
            vmem((NODES, 2 * WIDTH), F32),
            vmem((2, NODES, WIDTH), F32),
            vmem((2, NODES, WIDTH), F32),
            dma((9,)),
            dma((2,)),
            dma,
            dma,
            dma,
            dma,
            dma,
            dma((ITERS + 1, 4)),
            dma((ITERS + 1, 4)),
        ],
        compiler_params=pltpu.CompilerParams(
            collective_id=0, has_side_effects=True, vmem_limit_bytes=56 << 20
        ),
        name="newton_step",
    )(
        state,
        demand_load,
        node_coef,
        pipe_ends,
        pipe_coef,
        iface_node,
        jnp.transpose(iface_coef, (0, 2, 3, 1)),
        cons_node,
        cons_count.reshape(1, 1),
    )
    return step, resid


def solution(mesh):
    placed = (
        P(None, "dom", "samp"),
        P("samp", "dom", None),
        P(None, "dom"),
        P(None, "dom"),
        P(None, "dom"),
        P("dom", None, None),
        P(),
        P("dom", None),
        P("dom"),
    )
    return jax.shard_map(
        shards,
        mesh=mesh,
        in_specs=placed,
        out_specs=(P(None, "dom", "samp"), P(None, "dom", "samp")),
        check_vma=False,
    )
```

```python
import jax
import jax.numpy as jnp
from jax import lax
from jax.experimental import pallas as pl
from jax.experimental.pallas import tpu as pltpu
from jax.sharding import PartitionSpec as P

ITERS = 4
REACH = 4
MESH = pl.DeviceIdType.MESH
F32 = jnp.float32
BF16 = jnp.bfloat16

NODES = 256
PIPES = 512
IFACE = 64
FACES = 4 * IFACE
WIDTH = 128
SLOTS = 128
N_DOM = 128
HALF_DOM = N_DOM // 2
PARTNER_COLOUR = (1, 0, 3, 2)
DEEP = 8
FAR_FIRST_Z = (4, 3, 5, 2, 6, 1, 7, 0)
FAR_FIRST_X = (2, 1, 3, 0)


def split(value):
    high = value.astype(BF16)
    return high, (value - high.astype(F32)).astype(BF16)


def mm(table, value):
    return jnp.dot(table, value, preferred_element_type=F32)


def column(row):
    return jnp.transpose(jnp.broadcast_to(row, (WIDTH, row.shape[1])))


def two(left, right):
    return jnp.concatenate([left, right], axis=1)


def onehot(condition):
    return jnp.where(condition, F32(1.0), F32(0.0))


def pipe_terms(drop, temp_sum, temp_drop, conduct, spread):
    square = 1.0 + drop * drop
    half_power = lax.rsqrt(square)
    quarter = jnp.sqrt(half_power)
    flow = conduct * drop * quarter
    slope = conduct * (1.0 + 0.5 * drop * drop) * half_power * half_power * quarter
    under = flow * flow + spread * spread
    inverse = lax.rsqrt(under)
    half_flow = 0.5 * flow
    mixing = 0.5 * under * inverse
    heat = half_flow * temp_sum + mixing * temp_drop
    heat_slope = 0.5 * temp_sum + temp_drop * half_flow * inverse
    return flow, heat, slope, heat_slope * slope, half_flow, mixing


def kernel(
    state_hbm,
    demand_hbm,
    node_coef_hbm,
    pipe_ends_hbm,
    pipe_coef_hbm,
    iface_node_hbm,
    iface_coef_hbm,
    cons_node_hbm,
    cons_count_hbm,
    step_hbm,
    resid_hbm,
    state,
    demand,
    node_coef,
    pipe_ends,
    pipe_coef,
    iface_node,
    iface_coef,
    cons_node,
    cons_count,
    relay,
    rows_in,
    rows,
    faces_out,
    faces_in,
    m_nodes,
    a_nodes,
    m_pipes,
    a_pipes,
    f_nodes,
    f_faces,
    inner,
    outer,
    node,
    serves,
    high,
    low,
    pipe_high,
    pipe_low,
    face_high,
    face_low,
    extra_high,
    extra_low,
    mixed_both,
    rho,
    delta,
    step,
    resid,
    load_sem,
    out_sem,
    relay_send,
    relay_recv,
    rows_send,
    rows_self_send,
    rows_recv,
    face_send,
    face_recv,
):
    rank = lax.axis_index("dom")
    core = lax.axis_index("samp")
    owner_half = rank // HALF_DOM
    left = slice(0, WIDTH)
    right = slice(WIDTH, 2 * WIDTH)

    at_y, at_z, at_x = rank // 32, lax.rem(rank // REACH, DEEP), lax.rem(rank, REACH)

    def place(y, z, x):
        return 32 * y + REACH * z + x

    barrier = pltpu.get_barrier_semaphore()
    around = [lax.rem(rank + o + N_DOM, N_DOM) for o in (1, -1, REACH, -REACH)]
    for dz in FAR_FIRST_Z[:-1]:
        pl.semaphore_signal(
            barrier,
            inc=1,
            device_id=(place(at_y, lax.rem(at_z + dz, DEEP), at_x), core),
            device_id_type=MESH,
        )
    for dx in FAR_FIRST_X:
        for y in range(2):
            for c in range(2):
                source = place(2 * core + y, at_z, lax.rem(at_x + dx, REACH))
                pl.semaphore_signal(barrier, inc=1, device_id=(source, c), device_id_type=MESH)
    for q in around:
        pl.semaphore_signal(barrier, inc=1, device_id=(q, core), device_id_type=MESH)

    loads = [
        (iface_node_hbm, iface_node),
        (state_hbm, state),
        (demand_hbm, demand),
        (node_coef_hbm, node_coef),
        (pipe_ends_hbm, pipe_ends),
        (pipe_coef_hbm, pipe_coef),
        (cons_node_hbm, cons_node),
        (cons_count_hbm, cons_count),
        (iface_coef_hbm, iface_coef),
    ]
    loads = [
        pltpu.make_async_copy(src, dst, load_sem.at[i]) for i, (src, dst) in enumerate(loads)
    ]
    for load in loads:
        load.start()

    def chunk(i, size):
        return slice(i * size, (i + 1) * size)

    loads[0].wait()
    face_rows = [iface_node[0, c : c + 1, :].astype(F32) for c in range(4)]
    lane_of_node = lax.broadcasted_iota(jnp.int32, (IFACE, WIDTH), 1).astype(F32)
    for c in range(4):
        ids = column(face_rows[c])
        for part in range(NODES // WIDTH):
            f_faces[chunk(c, IFACE), chunk(part, WIDTH)] = onehot(
                ids == lane_of_node + float(part * WIDTH)
            ).astype(BF16)
    loads[1].wait()
    for i in range(2):
        for f in range(2):
            high[chunk(i, 128), chunk(f, WIDTH)], low[chunk(i, 128), chunk(f, WIDTH)] = split(
                state[f, chunk(i, 128), :]
            )

    def face_copies(turn):
        return [
            pltpu.make_async_remote_copy(
                src_ref=faces_out.at[turn, c],
                dst_ref=faces_in.at[turn, PARTNER_COLOUR[c]],
                send_sem=face_send.at[turn, c],
                recv_sem=face_recv.at[turn, PARTNER_COLOUR[c]],
                device_id=(around[c], core),
                device_id_type=MESH,
            )
            for c in range(4)
        ]

    def face_values(turn, c):
        table = f_faces[chunk(c, IFACE), :]
        faces_out[turn, c] = mm(table, high[...]) + mm(table, low[...])

    def pipe_drops(i):
        at = chunk(i, 128)
        drops = mm(m_pipes[at, :], high[...]) + mm(m_pipes[at, :], low[...])
        sums = mm(a_pipes[at, :], two(high[:, right], low[:, right]))
        return drops[:, left], drops[:, right], sums[:, left] + sums[:, right]

    copies = face_copies(0)
    for c in range(4):
        face_values(0, c)
    loads[2].wait()
    pl.semaphore_wait(barrier, DEEP - 1 + 16 + 4)

    def rows_of(y, z):
        return demand.at[0, :, pl.ds(pl.multiple_of(place(y, z, 0) * SLOTS, SLOTS), REACH * SLOTS)]

    for dz in FAR_FIRST_Z[:-1]:
        z = lax.rem(at_z + dz, DEEP)
        for y in range(4):
            pltpu.make_async_remote_copy(
                src_ref=rows_of(y, z),
                dst_ref=relay.at[at_z, y],
                send_sem=relay_send,
                recv_sem=relay_recv,
                device_id=(place(at_y, z, at_x), core),
                device_id_type=MESH,
            ).start()
    for copy in copies:
        copy.start()
    for y in range(4):
        pltpu.make_async_copy(rows_of(y, at_z), relay.at[at_z, y], relay_recv).start()

    for load in loads[3:]:
        load.wait()

    for i in range(NODES // 128):
        node_of_row = lax.broadcasted_iota(jnp.int32, (128, PIPES), 0) + i * 128
        at_start = onehot(pipe_ends[0:1, :] == node_of_row)
        at_end = onehot(pipe_ends[1:2, :] == node_of_row)
        m_nodes[chunk(i, 128), :] = (at_start - at_end).astype(BF16)
        a_nodes[chunk(i, 128), :] = (at_start + at_end).astype(BF16)
    lane_of_node = lax.broadcasted_iota(jnp.int32, (128, WIDTH), 1).astype(F32)
    for i in range(PIPES // 128):
        start_ids = column(pipe_ends[0:1, chunk(i, 128)].astype(F32))
        end_ids = column(pipe_ends[1:2, chunk(i, 128)].astype(F32))
        for part in range(NODES // WIDTH):
            at_start = onehot(start_ids == lane_of_node + float(part * WIDTH))
            at_end = onehot(end_ids == lane_of_node + float(part * WIDTH))
            m_pipes[chunk(i, 128), chunk(part, WIDTH)] = (at_start - at_end).astype(BF16)
            a_pipes[chunk(i, 128), chunk(part, WIDTH)] = (at_start + at_end).astype(BF16)
    face_ids = jnp.concatenate(face_rows, axis=1)
    for i in range(NODES // 128):
        node_of_row = lax.broadcasted_iota(jnp.int32, (128, FACES), 0) + i * 128
        f_nodes[chunk(i, 128), :] = onehot(face_ids == node_of_row.astype(F32)).astype(BF16)

    def scatter(table, i, upper, lower):
        return mm(table[chunk(i, 128), :], upper[...]) + mm(table[chunk(i, 128), :], lower[...])

    for i in range(PIPES // 128):
        at = chunk(i, 128)
        drop, temp_drop, temp_sum = pipe_drops(i)
        flow, heat, slope, mixed, half_flow, mixing = pipe_terms(
            drop, temp_sum, temp_drop, column(pipe_coef[0:1, at]), column(pipe_coef[1:2, at])
        )
        inner[0, at], inner[1, at], inner[2, at], inner[3, at] = slope, mixed, half_flow, mixing
        pipe_high[at, left], pipe_low[at, left] = split(flow)
        pipe_high[at, right], pipe_low[at, right] = split(heat)
        extra_high[at, left], extra_low[at, left] = split(slope)
        extra_high[at, right], extra_low[at, right] = split(mixing)
        mixed_both[at, left], mixed_both[at, right] = split(mixed)
    for i in range(NODES // 128):
        at = chunk(i, 128)
        rho[at, :] = scatter(m_nodes, i, pipe_high, pipe_low)
        slopes = scatter(a_nodes, i, extra_high, extra_low)
        cross = mm(a_nodes[at, :], mixed_both[...])
        node[0, at] = column(node_coef[0:1, at])
        node[1, at] = column(node_coef[1:2, at])
        node[2, at] = node[0, at] + slopes[:, left]
        node[3, at] = 0.5 * rho[at, left] + slopes[:, right]
        node[4, at] = cross[:, left] + cross[:, right]
        live = lax.broadcasted_iota(jnp.int32, (128, 2 * SLOTS), 1) < cons_count[...]
        here = cons_node[...] == lax.broadcasted_iota(jnp.int32, (128, 2 * SLOTS), 0) + i * 128
        serves[at, :] = onehot(jnp.logical_and(live, here)).astype(BF16)

    step[...] = jnp.zeros_like(step)

    lane = lax.broadcasted_iota(jnp.int32, (IFACE, N_DOM), 1)

    def iface_column(which, c):
        owner = (rank, around[1], rank, around[3])[c]
        mine = jnp.where(lane == owner, iface_coef[which, c // 2], F32(0.0))
        return jnp.broadcast_to(jnp.sum(mine, axis=1, keepdims=True), (IFACE, WIDTH))

    for c in range(4):
        outer[0, chunk(c, IFACE)] = iface_column(0, c)
        outer[1, chunk(c, IFACE)] = iface_column(1, c)
    pltpu.make_async_remote_copy(
        src_ref=relay,
        dst_ref=relay,
        send_sem=relay_send,
        recv_sem=relay_recv,
        device_id=(rank, 1 - core),
        device_id_type=MESH,
    ).wait_recv()
    group = core * 8 + lax.rem(at_y, 2) * REACH + at_x

    def relayed(y, x):
        return relay.at[:, y, :, pl.ds(pl.multiple_of(x * SLOTS, SLOTS), SLOTS)]

    for dy in FAR_FIRST_X:
        for dx in FAR_FIRST_X:
            if (dy, dx) != (0, 0):
                y, x = lax.rem(at_y + dy, 4), lax.rem(at_x + dx, REACH)
                pltpu.make_async_remote_copy(
                    src_ref=relayed(y, x),
                    dst_ref=rows_in.at[group],
                    send_sem=rows_send,
                    recv_sem=rows_recv,
                    device_id=(place(y, at_z, x), owner_half),
                    device_id_type=MESH,
                ).start()
    own_rows = relayed(at_y, at_x)

    @pl.when(owner_half == core)
    def _():
        pltpu.make_async_copy(own_rows, rows_in.at[group], rows_recv).start()

    across = pltpu.make_async_remote_copy(
        src_ref=own_rows,
        dst_ref=rows_in.at[group],
        send_sem=rows_self_send,
        recv_sem=rows_recv,
        device_id=(rank, 1 - core),
        device_id_type=MESH,
    )

    @pl.when(owner_half != core)
    def _():
        across.start()

    for copy in copies:
        copy.wait_recv()
    for c in range(4):
        at = chunk(c, IFACE)
        near_head, near_temp = faces_out[0, c, :, left], faces_out[0, c, :, right]
        far_head, far_temp = faces_in[0, c, :, left], faces_in[0, c, :, right]
        flow, heat, slope, mixed, half_flow, mixing = pipe_terms(
            near_head - far_head, near_temp + far_temp, near_temp - far_temp, outer[0, at], outer[1, at]
        )
        upper = half_flow + mixing
        outer[0, at], outer[1, at], outer[2, at], outer[3, at] = slope, mixed, upper, half_flow - mixing
        face_high[at, left], face_low[at, left] = split(flow)
        face_high[at, right], face_low[at, right] = split(heat)
        extra_high[at, left], extra_low[at, left] = split(slope)
        extra_high[at, right], extra_low[at, right] = split(upper)
        mixed_both[at, left], mixed_both[at, right] = split(mixed)
    for i in range(NODES // 128):
        at = chunk(i, 128)
        rho[at, :] += scatter(f_nodes, i, face_high, face_low)
        table = f_nodes[at, :]
        slopes = mm(table, extra_high[:FACES, :]) + mm(table, extra_low[:FACES, :])
        cross = mm(table, mixed_both[:FACES, :])
        node[2, at] = 1.0 / (node[2, at] + slopes[:, left])
        node[3, at] += slopes[:, right]
        node[4, at] += cross[:, left] + cross[:, right]

    def precondition(i):
        at = chunk(i, 128)
        head = -rho[at, left] * node[2, at]
        temp = -(rho[at, right] + node[4, at] * head) * node[3, at]
        delta[at, left] = head
        delta[at, right] = temp
        high[at, left], low[at, left] = split(head)
        high[at, right], low[at, right] = split(temp)

    pltpu.make_async_remote_copy(
        src_ref=rows_in,
        dst_ref=rows_in,
        send_sem=rows_send,
        recv_sem=rows_recv,
        device_id=(rank, 1 - core),
        device_id_type=MESH,
    ).wait_recv()
    for h in range(2):
        for y in range(2):
            for z in range(DEEP):
                for x in range(REACH):
                    rows[chunk(place(y, z, x), 2), chunk(h, SLOTS)] = rows_in[
                        h * 8 + y * REACH + x, z
                    ].astype(F32)
    for i in range(NODES // 128):
        at = chunk(i, 128)
        usage = lax.dot_general(
            serves[at, :],
            rows[...].astype(BF16),
            (((1,), (1,)), ((), ())),
            preferred_element_type=F32,
        )
        cooling = node[1, at] + usage
        node[1, at] = cooling
        node[3, at] = 1.0 / (node[3, at] + cooling)
        rho[at, left] += node[0, at] * state[0, at] + usage
        rho[at, right] += cooling * state[1, at]
        resid[0, at] = rho[at, left]
        resid[1, at] = rho[at, right]
        precondition(i)

    resid_out = pltpu.make_async_copy(resid, resid_hbm, out_sem.at[0])
    resid_out.start()

    def one_turn(turn, carry):
        copies = face_copies(turn)
        for c in range(4):
            face_values(turn, c)
            copies[c].start()
        for i in range(PIPES // 128):
            at = chunk(i, 128)
            drop, temp_drop, temp_sum = pipe_drops(i)
            pipe_high[at, left], pipe_low[at, left] = split(inner[0, at] * drop)
            pipe_high[at, right], pipe_low[at, right] = split(
                inner[1, at] * drop + inner[2, at] * temp_sum + inner[3, at] * temp_drop
            )
        for c in range(4):
            at = chunk(c, IFACE)
            head, temp = faces_out[turn, c, :, left], faces_out[turn, c, :, right]
            face_high[at, left], face_low[at, left] = split(outer[0, at] * head)
            face_high[at, right], face_low[at, right] = split(outer[1, at] * head + outer[2, at] * temp)
        for i in range(NODES // 128):
            at = chunk(i, 128)
            moved = scatter(m_nodes, i, pipe_high, pipe_low) + scatter(f_nodes, i, face_high, face_low)
            head, temp = delta[at, left], delta[at, right]
            rho[at, left] += moved[:, left] + node[0, at] * head
            rho[at, right] += moved[:, right] + node[1, at] * temp
            step[0, at] += head
            step[1, at] += temp
        for copy in copies:
            copy.wait_recv()
        for c in range(4):
            at = chunk(c, IFACE)
            head, temp = faces_in[turn, c, :, left], faces_in[turn, c, :, right]
            face_high[at, left], face_low[at, left] = split(-outer[0, at] * head)
            face_high[at, right], face_low[at, right] = split(outer[3, at] * temp - outer[1, at] * head)
        for i in range(NODES // 128):
            at = chunk(i, 128)
            rho[at, :] += scatter(f_nodes, i, face_high, face_low)
            precondition(i)
        return carry

    lax.fori_loop(1, ITERS + 1, one_turn, 0)
    for i in range(NODES // 128):
        at = chunk(i, 128)
        step[0, at] += delta[at, left]
        step[1, at] += delta[at, right]
    step_out = pltpu.make_async_copy(step, step_hbm, out_sem.at[1])
    step_out.start()

    def sent(turn, carry):
        for copy in face_copies(turn):
            copy.wait_send()
        return carry

    lax.fori_loop(0, ITERS + 1, sent, 0)
    pltpu.make_async_remote_copy(
        src_ref=relay.at[pl.ds(0, DEEP - 1)],
        dst_ref=relay.at[pl.ds(0, DEEP - 1)],
        send_sem=relay_send,
        recv_sem=relay_recv,
        device_id=(rank, 1 - core),
        device_id_type=MESH,
    ).wait_send()
    pltpu.make_async_remote_copy(
        src_ref=rows_in.at[pl.ds(0, 15)],
        dst_ref=rows_in.at[pl.ds(0, 15)],
        send_sem=rows_send,
        recv_sem=rows_recv,
        device_id=(rank, 1 - core),
        device_id_type=MESH,
    ).wait_send()

    @pl.when(owner_half != core)
    def _():
        across.wait_send()

    resid_out.wait()
    step_out.wait()


def write_out(step_in, resid_in, step_out, resid_out, stage, in_sem, out_sem):
    pairs = [(resid_in, resid_out, 0), (resid_in, resid_out, 1), (step_in, step_out, 0), (step_in, step_out, 1)]
    fetches = [
        pltpu.make_async_copy(src.at[f], stage.at[i], in_sem.at[i])
        for i, (src, _, f) in enumerate(pairs)
    ]
    stores = [
        pltpu.make_async_copy(stage.at[i], dst.at[f], out_sem.at[i])
        for i, (_, dst, f) in enumerate(pairs)
    ]
    for fetch in fetches:
        fetch.start()
    for fetch, store in zip(fetches, stores):
        fetch.wait()
        store.start()
    for store in stores:
        store.wait()


def shards(
    state,
    demand_load,
    node_coef,
    pipe_ends,
    pipe_coef,
    iface_node,
    iface_coef,
    cons_node,
    cons_count,
):
    vmem = pltpu.VMEM
    dma = pltpu.SemaphoreType.DMA
    anywhere = pl.BlockSpec(memory_space=pl.ANY)
    out = jax.ShapeDtypeStruct((2, NODES, WIDTH), F32)
    step, resid = pl.pallas_call(
        kernel,
        out_shape=(out, out),
        in_specs=[anywhere] * 9,
        out_specs=(anywhere, anywhere),
        scratch_shapes=[
            vmem((2, NODES, WIDTH), F32),
            vmem((1, 2, N_DOM * SLOTS), BF16),
            vmem((2, NODES), F32),
            vmem((2, PIPES), jnp.int32),
            vmem((2, PIPES), F32),
            vmem((1, 4, IFACE), jnp.int32),
            vmem((2, 2, IFACE, N_DOM), F32),
            vmem((1, 2 * SLOTS), jnp.int32),
            vmem((1, 1), jnp.int32),
            vmem((DEEP, 4, 2, REACH * SLOTS), BF16),
            vmem((16, DEEP, 2, SLOTS), BF16),
            vmem((WIDTH, 2 * SLOTS), F32),
            vmem((ITERS + 1, 4, IFACE, 2 * WIDTH), F32),
            vmem((ITERS + 1, 4, IFACE, 2 * WIDTH), F32),
            vmem((NODES, PIPES), BF16),
            vmem((NODES, PIPES), BF16),
            vmem((PIPES, NODES), BF16),
            vmem((PIPES, NODES), BF16),
            vmem((NODES, FACES), BF16),
            vmem((FACES, NODES), BF16),
            vmem((4, PIPES, WIDTH), F32),
            vmem((4, FACES, WIDTH), F32),
            vmem((5, NODES, WIDTH), F32),
            vmem((NODES, 2 * SLOTS), BF16),
            vmem((NODES, 2 * WIDTH), BF16),
            vmem((NODES, 2 * WIDTH), BF16),
            vmem((PIPES, 2 * WIDTH), BF16),
            vmem((PIPES, 2 * WIDTH), BF16),
            vmem((FACES, 2 * WIDTH), BF16),
            vmem((FACES, 2 * WIDTH), BF16),
            vmem((PIPES, 2 * WIDTH), BF16),
            vmem((PIPES, 2 * WIDTH), BF16),
            vmem((PIPES, 2 * WIDTH), BF16),
            vmem((NODES, 2 * WIDTH), F32),
            vmem((NODES, 2 * WIDTH), F32),
            vmem((2, NODES, WIDTH), F32),
            vmem((2, NODES, WIDTH), F32),
            dma((9,)),
            dma((2,)),
            dma,
            dma,
            dma,
            dma,
            dma,
            dma((ITERS + 1, 4)),
            dma((ITERS + 1, 4)),
        ],
        compiler_params=pltpu.CompilerParams(
            collective_id=0, has_side_effects=True, vmem_limit_bytes=56 << 20
        ),
        name="newton_step",
    )(
        state,
        demand_load,
        node_coef,
        pipe_ends,
        pipe_coef,
        iface_node,
        jnp.transpose(iface_coef, (0, 2, 3, 1)),
        cons_node,
        cons_count.reshape(1, 1),
    )
    step, resid = pl.pallas_call(
        write_out,
        out_shape=(out, out),
        in_specs=[anywhere] * 2,
        out_specs=(anywhere, anywhere),
        scratch_shapes=[
            vmem((4, NODES, WIDTH), F32),
            dma((4,)),
            dma((4,)),
        ],
        compiler_params=pltpu.CompilerParams(vmem_limit_bytes=56 << 20),
        name="write_out",
    )(step, resid)
    return step, resid


def solution(mesh):
    placed = (
        P(None, "dom", "samp"),
        P("samp", "dom", None),
        P(None, "dom"),
        P(None, "dom"),
        P(None, "dom"),
        P("dom", None, None),
        P(),
        P("dom", None),
        P("dom"),
    )
    return jax.shard_map(
        shards,
        mesh=mesh,
        in_specs=placed,
        out_specs=(P(None, "dom", "samp"), P(None, "dom", "samp")),
        check_vma=False,
    )
```

```python
import jax
import jax.numpy as jnp
from jax import lax
from jax.experimental import pallas as pl
from jax.experimental.pallas import tpu as pltpu
from jax.sharding import PartitionSpec as P

ITERS = 4
REACH = 4
MESH = pl.DeviceIdType.MESH
F32 = jnp.float32
BF16 = jnp.bfloat16

NODES = 256
PIPES = 512
IFACE = 64
FACES = 4 * IFACE
WIDTH = 128
SLOTS = 128
N_DOM = 128
HALF_DOM = N_DOM // 2
PARTNER_COLOUR = (1, 0, 3, 2)
DEEP = 8
FAR_FIRST_Z = (4, 3, 5, 2, 6, 1, 7, 0)
FAR_FIRST_X = (2, 1, 3, 0)


def split(value):
    high = value.astype(BF16)
    return high, (value - high.astype(F32)).astype(BF16)


def mm(table, value):
    return jnp.dot(table, value, preferred_element_type=F32)


def column(row):
    return jnp.transpose(jnp.broadcast_to(row, (WIDTH, row.shape[1])))


def two(left, right):
    return jnp.concatenate([left, right], axis=1)


def onehot(condition):
    return jnp.where(condition, F32(1.0), F32(0.0))


def pipe_terms(drop, temp_sum, temp_drop, conduct, spread):
    square = 1.0 + drop * drop
    half_power = lax.rsqrt(square)
    quarter = jnp.sqrt(half_power)
    flow = conduct * drop * quarter
    slope = conduct * (1.0 + 0.5 * drop * drop) * half_power * half_power * quarter
    under = flow * flow + spread * spread
    inverse = lax.rsqrt(under)
    half_flow = 0.5 * flow
    mixing = 0.5 * under * inverse
    heat = half_flow * temp_sum + mixing * temp_drop
    heat_slope = 0.5 * temp_sum + temp_drop * half_flow * inverse
    return flow, heat, slope, heat_slope * slope, half_flow, mixing


def kernel(
    state_hbm,
    demand_hbm,
    node_coef_hbm,
    pipe_ends_hbm,
    pipe_coef_hbm,
    iface_node_hbm,
    iface_coef_hbm,
    cons_node_hbm,
    cons_count_hbm,
    step_hbm,
    resid_hbm,
    state,
    demand,
    node_coef,
    pipe_ends,
    pipe_coef,
    iface_node,
    iface_coef,
    cons_node,
    cons_count,
    relay,
    rows_in,
    rows,
    faces_out,
    faces_in,
    m_nodes,
    a_nodes,
    m_pipes,
    a_pipes,
    f_nodes,
    f_faces,
    inner,
    outer,
    node,
    serves,
    high,
    low,
    pipe_high,
    pipe_low,
    face_high,
    face_low,
    extra_high,
    extra_low,
    mixed_both,
    rho,
    delta,
    step,
    resid,
    load_sem,
    out_sem,
    relay_send,
    relay_recv,
    rows_send,
    rows_self_send,
    rows_recv,
    face_send,
    face_recv,
):
    rank = lax.axis_index("dom")
    core = lax.axis_index("samp")
    owner_half = rank // HALF_DOM
    left = slice(0, WIDTH)
    right = slice(WIDTH, 2 * WIDTH)

    at_y, at_z, at_x = rank // 32, lax.rem(rank // REACH, DEEP), lax.rem(rank, REACH)

    def place(y, z, x):
        return 32 * y + REACH * z + x

    barrier = pltpu.get_barrier_semaphore()
    around = [lax.rem(rank + o + N_DOM, N_DOM) for o in (1, -1, REACH, -REACH)]
    for dz in FAR_FIRST_Z[:-1]:
        pl.semaphore_signal(
            barrier,
            inc=1,
            device_id=(place(at_y, lax.rem(at_z + dz, DEEP), at_x), core),
            device_id_type=MESH,
        )
    for dx in FAR_FIRST_X:
        for y in range(2):
            for c in range(2):
                source = place(2 * core + y, at_z, lax.rem(at_x + dx, REACH))
                pl.semaphore_signal(barrier, inc=1, device_id=(source, c), device_id_type=MESH)
    for q in around:
        pl.semaphore_signal(barrier, inc=1, device_id=(q, core), device_id_type=MESH)

    loads = [
        (iface_node_hbm, iface_node),
        (state_hbm, state),
        (demand_hbm, demand),
        (node_coef_hbm, node_coef),
        (pipe_ends_hbm, pipe_ends),
        (pipe_coef_hbm, pipe_coef),
        (cons_node_hbm, cons_node),
        (cons_count_hbm, cons_count),
        (iface_coef_hbm, iface_coef),
    ]
    loads = [
        pltpu.make_async_copy(src, dst, load_sem.at[i]) for i, (src, dst) in enumerate(loads)
    ]
    for load in loads:
        load.start()

    def chunk(i, size):
        return slice(i * size, (i + 1) * size)

    loads[0].wait()
    face_rows = [iface_node[0, c : c + 1, :].astype(F32) for c in range(4)]
    lane_of_node = lax.broadcasted_iota(jnp.int32, (IFACE, WIDTH), 1).astype(F32)
    for c in range(4):
        ids = column(face_rows[c])
        for part in range(NODES // WIDTH):
            f_faces[chunk(c, IFACE), chunk(part, WIDTH)] = onehot(
                ids == lane_of_node + float(part * WIDTH)
            ).astype(BF16)
    loads[1].wait()
    for i in range(2):
        for f in range(2):
            high[chunk(i, 128), chunk(f, WIDTH)], low[chunk(i, 128), chunk(f, WIDTH)] = split(
                state[f, chunk(i, 128), :]
            )

    def face_copies(turn):
        return [
            pltpu.make_async_remote_copy(
                src_ref=faces_out.at[turn, c],
                dst_ref=faces_in.at[turn, PARTNER_COLOUR[c]],
                send_sem=face_send.at[turn, c],
                recv_sem=face_recv.at[turn, PARTNER_COLOUR[c]],
                device_id=(around[c], core),
                device_id_type=MESH,
            )
            for c in range(4)
        ]

    def face_values(turn, c):
        table = f_faces[chunk(c, IFACE), :]
        faces_out[turn, c] = mm(table, high[...]) + mm(table, low[...])

    def pipe_drops(i):
        at = chunk(i, 128)
        drops = mm(m_pipes[at, :], high[...]) + mm(m_pipes[at, :], low[...])
        sums = mm(a_pipes[at, :], two(high[:, right], low[:, right]))
        return drops[:, left], drops[:, right], sums[:, left] + sums[:, right]

    copies = face_copies(0)
    for c in range(4):
        face_values(0, c)
    loads[2].wait()
    pl.semaphore_wait(barrier, DEEP - 1 + 16 + 4)

    def rows_of(y, z):
        return demand.at[0, :, pl.ds(pl.multiple_of(place(y, z, 0) * SLOTS, SLOTS), REACH * SLOTS)]

    for dz in FAR_FIRST_Z[:-1]:
        z = lax.rem(at_z + dz, DEEP)
        for y in range(4):
            pltpu.make_async_remote_copy(
                src_ref=rows_of(y, z),
                dst_ref=relay.at[at_z, y],
                send_sem=relay_send,
                recv_sem=relay_recv,
                device_id=(place(at_y, z, at_x), core),
                device_id_type=MESH,
            ).start()
    for copy in copies:
        copy.start()
    for y in range(4):
        pltpu.make_async_copy(rows_of(y, at_z), relay.at[at_z, y], relay_recv).start()

    for load in loads[3:]:
        load.wait()

    for i in range(NODES // 128):
        node_of_row = lax.broadcasted_iota(jnp.int32, (128, PIPES), 0) + i * 128
        at_start = onehot(pipe_ends[0:1, :] == node_of_row)
        at_end = onehot(pipe_ends[1:2, :] == node_of_row)
        m_nodes[chunk(i, 128), :] = (at_start - at_end).astype(BF16)
        a_nodes[chunk(i, 128), :] = (at_start + at_end).astype(BF16)
    lane_of_node = lax.broadcasted_iota(jnp.int32, (128, WIDTH), 1).astype(F32)
    for i in range(PIPES // 128):
        start_ids = column(pipe_ends[0:1, chunk(i, 128)].astype(F32))
        end_ids = column(pipe_ends[1:2, chunk(i, 128)].astype(F32))
        for part in range(NODES // WIDTH):
            at_start = onehot(start_ids == lane_of_node + float(part * WIDTH))
            at_end = onehot(end_ids == lane_of_node + float(part * WIDTH))
            m_pipes[chunk(i, 128), chunk(part, WIDTH)] = (at_start - at_end).astype(BF16)
            a_pipes[chunk(i, 128), chunk(part, WIDTH)] = (at_start + at_end).astype(BF16)
    face_ids = jnp.concatenate(face_rows, axis=1)
    for i in range(NODES // 128):
        node_of_row = lax.broadcasted_iota(jnp.int32, (128, FACES), 0) + i * 128
        f_nodes[chunk(i, 128), :] = onehot(face_ids == node_of_row.astype(F32)).astype(BF16)

    def scatter(table, i, upper, lower):
        return mm(table[chunk(i, 128), :], upper[...]) + mm(table[chunk(i, 128), :], lower[...])

    for i in range(PIPES // 128):
        at = chunk(i, 128)
        drop, temp_drop, temp_sum = pipe_drops(i)
        flow, heat, slope, mixed, half_flow, mixing = pipe_terms(
            drop, temp_sum, temp_drop, column(pipe_coef[0:1, at]), column(pipe_coef[1:2, at])
        )
        inner[0, at], inner[1, at], inner[2, at], inner[3, at] = slope, mixed, half_flow, mixing
        pipe_high[at, left], pipe_low[at, left] = split(flow)
        pipe_high[at, right], pipe_low[at, right] = split(heat)
        extra_high[at, left], extra_low[at, left] = split(slope)
        extra_high[at, right], extra_low[at, right] = split(mixing)
        mixed_both[at, left], mixed_both[at, right] = split(mixed)
    for i in range(NODES // 128):
        at = chunk(i, 128)
        rho[at, :] = scatter(m_nodes, i, pipe_high, pipe_low)
        slopes = scatter(a_nodes, i, extra_high, extra_low)
        cross = mm(a_nodes[at, :], mixed_both[...])
        node[0, at] = column(node_coef[0:1, at])
        node[1, at] = column(node_coef[1:2, at])
        node[2, at] = node[0, at] + slopes[:, left]
        node[3, at] = 0.5 * rho[at, left] + slopes[:, right]
        node[4, at] = cross[:, left] + cross[:, right]
        live = lax.broadcasted_iota(jnp.int32, (128, 2 * SLOTS), 1) < cons_count[...]
        here = cons_node[...] == lax.broadcasted_iota(jnp.int32, (128, 2 * SLOTS), 0) + i * 128
        serves[at, :] = onehot(jnp.logical_and(live, here)).astype(BF16)

    step[...] = jnp.zeros_like(step)

    lane = lax.broadcasted_iota(jnp.int32, (IFACE, N_DOM), 1)

    def iface_column(which, c):
        owner = (rank, around[1], rank, around[3])[c]
        mine = jnp.where(lane == owner, iface_coef[which, c // 2], F32(0.0))
        return jnp.broadcast_to(jnp.sum(mine, axis=1, keepdims=True), (IFACE, WIDTH))

    for c in range(4):
        outer[0, chunk(c, IFACE)] = iface_column(0, c)
        outer[1, chunk(c, IFACE)] = iface_column(1, c)
    pltpu.make_async_remote_copy(
        src_ref=relay,
        dst_ref=relay,
        send_sem=relay_send,
        recv_sem=relay_recv,
        device_id=(rank, 1 - core),
        device_id_type=MESH,
    ).wait_recv()
    group = core * 8 + lax.rem(at_y, 2) * REACH + at_x

    def relayed(y, x):
        return relay.at[:, y, :, pl.ds(pl.multiple_of(x * SLOTS, SLOTS), SLOTS)]

    for dy in FAR_FIRST_X:
        for dx in FAR_FIRST_X:
            if (dy, dx) != (0, 0):
                y, x = lax.rem(at_y + dy, 4), lax.rem(at_x + dx, REACH)
                pltpu.make_async_remote_copy(
                    src_ref=relayed(y, x),
                    dst_ref=rows_in.at[group],
                    send_sem=rows_send,
                    recv_sem=rows_recv,
                    device_id=(place(y, at_z, x), owner_half),
                    device_id_type=MESH,
                ).start()
    own_rows = relayed(at_y, at_x)

    @pl.when(owner_half == core)
    def _():
        pltpu.make_async_copy(own_rows, rows_in.at[group], rows_recv).start()

    across = pltpu.make_async_remote_copy(
        src_ref=own_rows,
        dst_ref=rows_in.at[group],
        send_sem=rows_self_send,
        recv_sem=rows_recv,
        device_id=(rank, 1 - core),
        device_id_type=MESH,
    )

    @pl.when(owner_half != core)
    def _():
        across.start()

    for copy in copies:
        copy.wait_recv()
    for c in range(4):
        at = chunk(c, IFACE)
        near_head, near_temp = faces_out[0, c, :, left], faces_out[0, c, :, right]
        far_head, far_temp = faces_in[0, c, :, left], faces_in[0, c, :, right]
        flow, heat, slope, mixed, half_flow, mixing = pipe_terms(
            near_head - far_head, near_temp + far_temp, near_temp - far_temp, outer[0, at], outer[1, at]
        )
        upper = half_flow + mixing
        outer[0, at], outer[1, at], outer[2, at], outer[3, at] = slope, mixed, upper, half_flow - mixing
        face_high[at, left], face_low[at, left] = split(flow)
        face_high[at, right], face_low[at, right] = split(heat)
        extra_high[at, left], extra_low[at, left] = split(slope)
        extra_high[at, right], extra_low[at, right] = split(upper)
        mixed_both[at, left], mixed_both[at, right] = split(mixed)
    for i in range(NODES // 128):
        at = chunk(i, 128)
        rho[at, :] += scatter(f_nodes, i, face_high, face_low)
        table = f_nodes[at, :]
        slopes = mm(table, extra_high[:FACES, :]) + mm(table, extra_low[:FACES, :])
        cross = mm(table, mixed_both[:FACES, :])
        node[2, at] = 1.0 / (node[2, at] + slopes[:, left])
        node[3, at] += slopes[:, right]
        node[4, at] += cross[:, left] + cross[:, right]

    def precondition(i):
        at = chunk(i, 128)
        head = -rho[at, left] * node[2, at]
        temp = -(rho[at, right] + node[4, at] * head) * node[3, at]
        delta[at, left] = head
        delta[at, right] = temp
        high[at, left], low[at, left] = split(head)
        high[at, right], low[at, right] = split(temp)

    pltpu.make_async_remote_copy(
        src_ref=rows_in,
        dst_ref=rows_in,
        send_sem=rows_send,
        recv_sem=rows_recv,
        device_id=(rank, 1 - core),
        device_id_type=MESH,
    ).wait_recv()
    for h in range(2):
        for y in range(2):
            for z in range(DEEP):
                for x in range(REACH):
                    rows[chunk(place(y, z, x), 2), chunk(h, SLOTS)] = rows_in[
                        h * 8 + y * REACH + x, z
                    ].astype(F32)
    for i in range(NODES // 128):
        at = chunk(i, 128)
        usage = lax.dot_general(
            serves[at, :],
            rows[...].astype(BF16),
            (((1,), (1,)), ((), ())),
            preferred_element_type=F32,
        )
        cooling = node[1, at] + usage
        node[1, at] = cooling
        node[3, at] = 1.0 / (node[3, at] + cooling)
        rho[at, left] += node[0, at] * state[0, at] + usage
        rho[at, right] += cooling * state[1, at]
        resid[0, at] = rho[at, left]
        resid[1, at] = rho[at, right]
        precondition(i)

    resid_out = pltpu.make_async_copy(resid, resid_hbm, out_sem.at[0])
    resid_out.start()

    wraps_x = (at_x == 0).astype(jnp.int32)
    wraps_z = (at_z == 0).astype(jnp.int32)
    leaving = [
        (colour, lax.rem(rank + (1 - 2 * lax.rem(colour, 2)) * reach + N_DOM, N_DOM))
        for colour, reach in (
            (wraps_x, 1),
            (2 + wraps_z, REACH),
            (1 - wraps_x, 1),
            (3 - wraps_z, REACH),
        )
    ]

    def one_turn(turn, carry):
        copies = face_copies(turn)
        for colour, target in leaving:
            table = f_faces[pl.ds(pl.multiple_of(colour * IFACE, IFACE), IFACE), :]
            faces_out[turn, colour] = mm(table, high[...]) + mm(table, low[...])
            pltpu.make_async_remote_copy(
                src_ref=faces_out.at[turn, colour],
                dst_ref=faces_in.at[turn, colour + 1 - 2 * lax.rem(colour, 2)],
                send_sem=face_send.at[turn, colour],
                recv_sem=face_recv.at[turn, colour + 1 - 2 * lax.rem(colour, 2)],
                device_id=(target, core),
                device_id_type=MESH,
            ).start()
        for i in range(PIPES // 128):
            at = chunk(i, 128)
            drop, temp_drop, temp_sum = pipe_drops(i)
            pipe_high[at, left], pipe_low[at, left] = split(inner[0, at] * drop)
            pipe_high[at, right], pipe_low[at, right] = split(
                inner[1, at] * drop + inner[2, at] * temp_sum + inner[3, at] * temp_drop
            )
        for c in range(4):
            at = chunk(c, IFACE)
            head, temp = faces_out[turn, c, :, left], faces_out[turn, c, :, right]
            face_high[at, left], face_low[at, left] = split(outer[0, at] * head)
            face_high[at, right], face_low[at, right] = split(outer[1, at] * head + outer[2, at] * temp)
        for i in range(NODES // 128):
            at = chunk(i, 128)
            moved = scatter(m_nodes, i, pipe_high, pipe_low) + scatter(f_nodes, i, face_high, face_low)
            head, temp = delta[at, left], delta[at, right]
            rho[at, left] += moved[:, left] + node[0, at] * head
            rho[at, right] += moved[:, right] + node[1, at] * temp
            step[0, at] += head
            step[1, at] += temp
        for copy in copies:
            copy.wait_recv()
        for c in range(4):
            at = chunk(c, IFACE)
            head, temp = faces_in[turn, c, :, left], faces_in[turn, c, :, right]
            face_high[at, left], face_low[at, left] = split(-outer[0, at] * head)
            face_high[at, right], face_low[at, right] = split(outer[3, at] * temp - outer[1, at] * head)
        for i in range(NODES // 128):
            at = chunk(i, 128)
            rho[at, :] += scatter(f_nodes, i, face_high, face_low)
            precondition(i)
        return carry

    lax.fori_loop(1, ITERS + 1, one_turn, 0)
    for i in range(NODES // 128):
        at = chunk(i, 128)
        step[0, at] += delta[at, left]
        step[1, at] += delta[at, right]
    step_out = pltpu.make_async_copy(step, step_hbm, out_sem.at[1])
    step_out.start()

    def sent(turn, carry):
        for copy in face_copies(turn):
            copy.wait_send()
        return carry

    lax.fori_loop(0, ITERS + 1, sent, 0)
    pltpu.make_async_remote_copy(
        src_ref=relay.at[pl.ds(0, DEEP - 1)],
        dst_ref=relay.at[pl.ds(0, DEEP - 1)],
        send_sem=relay_send,
        recv_sem=relay_recv,
        device_id=(rank, 1 - core),
        device_id_type=MESH,
    ).wait_send()
    pltpu.make_async_remote_copy(
        src_ref=rows_in.at[pl.ds(0, 15)],
        dst_ref=rows_in.at[pl.ds(0, 15)],
        send_sem=rows_send,
        recv_sem=rows_recv,
        device_id=(rank, 1 - core),
        device_id_type=MESH,
    ).wait_send()

    @pl.when(owner_half != core)
    def _():
        across.wait_send()

    resid_out.wait()
    step_out.wait()


def write_out(step_in, resid_in, step_out, resid_out, stage, in_sem, out_sem):
    pairs = [(resid_in, resid_out, 0), (resid_in, resid_out, 1), (step_in, step_out, 0), (step_in, step_out, 1)]
    fetches = [
        pltpu.make_async_copy(src.at[f], stage.at[i], in_sem.at[i])
        for i, (src, _, f) in enumerate(pairs)
    ]
    stores = [
        pltpu.make_async_copy(stage.at[i], dst.at[f], out_sem.at[i])
        for i, (_, dst, f) in enumerate(pairs)
    ]
    for fetch in fetches:
        fetch.start()
    for fetch, store in zip(fetches, stores):
        fetch.wait()
        store.start()
    for store in stores:
        store.wait()


def shards(
    state,
    demand_load,
    node_coef,
    pipe_ends,
    pipe_coef,
    iface_node,
    iface_coef,
    cons_node,
    cons_count,
):
    vmem = pltpu.VMEM
    dma = pltpu.SemaphoreType.DMA
    anywhere = pl.BlockSpec(memory_space=pl.ANY)
    out = jax.ShapeDtypeStruct((2, NODES, WIDTH), F32)
    step, resid = pl.pallas_call(
        kernel,
        out_shape=(out, out),
        in_specs=[anywhere] * 9,
        out_specs=(anywhere, anywhere),
        scratch_shapes=[
            vmem((2, NODES, WIDTH), F32),
            vmem((1, 2, N_DOM * SLOTS), BF16),
            vmem((2, NODES), F32),
            vmem((2, PIPES), jnp.int32),
            vmem((2, PIPES), F32),
            vmem((1, 4, IFACE), jnp.int32),
            vmem((2, 2, IFACE, N_DOM), F32),
            vmem((1, 2 * SLOTS), jnp.int32),
            vmem((1, 1), jnp.int32),
            vmem((DEEP, 4, 2, REACH * SLOTS), BF16),
            vmem((16, DEEP, 2, SLOTS), BF16),
            vmem((WIDTH, 2 * SLOTS), F32),
            vmem((ITERS + 1, 4, IFACE, 2 * WIDTH), F32),
            vmem((ITERS + 1, 4, IFACE, 2 * WIDTH), F32),
            vmem((NODES, PIPES), BF16),
            vmem((NODES, PIPES), BF16),
            vmem((PIPES, NODES), BF16),
            vmem((PIPES, NODES), BF16),
            vmem((NODES, FACES), BF16),
            vmem((FACES, NODES), BF16),
            vmem((4, PIPES, WIDTH), F32),
            vmem((4, FACES, WIDTH), F32),
            vmem((5, NODES, WIDTH), F32),
            vmem((NODES, 2 * SLOTS), BF16),
            vmem((NODES, 2 * WIDTH), BF16),
            vmem((NODES, 2 * WIDTH), BF16),
            vmem((PIPES, 2 * WIDTH), BF16),
            vmem((PIPES, 2 * WIDTH), BF16),
            vmem((FACES, 2 * WIDTH), BF16),
            vmem((FACES, 2 * WIDTH), BF16),
            vmem((PIPES, 2 * WIDTH), BF16),
            vmem((PIPES, 2 * WIDTH), BF16),
            vmem((PIPES, 2 * WIDTH), BF16),
            vmem((NODES, 2 * WIDTH), F32),
            vmem((NODES, 2 * WIDTH), F32),
            vmem((2, NODES, WIDTH), F32),
            vmem((2, NODES, WIDTH), F32),
            dma((9,)),
            dma((2,)),
            dma,
            dma,
            dma,
            dma,
            dma,
            dma((ITERS + 1, 4)),
            dma((ITERS + 1, 4)),
        ],
        compiler_params=pltpu.CompilerParams(
            collective_id=0, has_side_effects=True, vmem_limit_bytes=56 << 20
        ),
        name="newton_step",
    )(
        state,
        demand_load,
        node_coef,
        pipe_ends,
        pipe_coef,
        iface_node,
        jnp.transpose(iface_coef, (0, 2, 3, 1)),
        cons_node,
        cons_count.reshape(1, 1),
    )
    step, resid = pl.pallas_call(
        write_out,
        out_shape=(out, out),
        in_specs=[anywhere] * 2,
        out_specs=(anywhere, anywhere),
        scratch_shapes=[
            vmem((4, NODES, WIDTH), F32),
            dma((4,)),
            dma((4,)),
        ],
        compiler_params=pltpu.CompilerParams(vmem_limit_bytes=56 << 20),
        name="write_out",
    )(step, resid)
    return step, resid


def solution(mesh):
    placed = (
        P(None, "dom", "samp"),
        P("samp", "dom", None),
        P(None, "dom"),
        P(None, "dom"),
        P(None, "dom"),
        P("dom", None, None),
        P(),
        P("dom", None),
        P("dom"),
    )
    return jax.shard_map(
        shards,
        mesh=mesh,
        in_specs=placed,
        out_specs=(P(None, "dom", "samp"), P(None, "dom", "samp")),
        check_vma=False,
    )
```

```python
import jax
import jax.numpy as jnp
from jax import lax
from jax.experimental import pallas as pl
from jax.experimental.pallas import tpu as pltpu
from jax.sharding import PartitionSpec as P

ITERS = 4
REACH = 4
MESH = pl.DeviceIdType.MESH
F32 = jnp.float32
BF16 = jnp.bfloat16

NODES = 256
PIPES = 512
IFACE = 64
FACES = 4 * IFACE
WIDTH = 128
SLOTS = 128
N_DOM = 128
HALF_DOM = N_DOM // 2
PARTNER_COLOUR = (1, 0, 3, 2)
DEEP = 8
FAR_FIRST_Z = (4, 3, 5, 2, 6, 1, 7, 0)
FAR_FIRST_X = (2, 1, 3, 0)


def split(value):
    high = value.astype(BF16)
    return high, (value - high.astype(F32)).astype(BF16)


def mm(table, value):
    return jnp.dot(table, value, preferred_element_type=F32)


def column(row):
    return jnp.transpose(jnp.broadcast_to(row, (WIDTH, row.shape[1])))


def two(left, right):
    return jnp.concatenate([left, right], axis=1)


def onehot(condition):
    return jnp.where(condition, F32(1.0), F32(0.0))


def pipe_terms(drop, temp_sum, temp_drop, conduct, spread):
    square = 1.0 + drop * drop
    half_power = lax.rsqrt(square)
    quarter = jnp.sqrt(half_power)
    flow = conduct * drop * quarter
    slope = conduct * (1.0 + 0.5 * drop * drop) * half_power * half_power * quarter
    under = flow * flow + spread * spread
    inverse = lax.rsqrt(under)
    half_flow = 0.5 * flow
    mixing = 0.5 * under * inverse
    heat = half_flow * temp_sum + mixing * temp_drop
    heat_slope = 0.5 * temp_sum + temp_drop * half_flow * inverse
    return flow, heat, slope, heat_slope * slope, half_flow, mixing


def kernel(
    state_hbm,
    demand_hbm,
    node_coef_hbm,
    pipe_ends_hbm,
    pipe_coef_hbm,
    iface_node_hbm,
    iface_coef_hbm,
    cons_node_hbm,
    cons_count_hbm,
    step_hbm,
    resid_hbm,
    state,
    demand,
    node_coef,
    pipe_ends,
    pipe_coef,
    iface_node,
    iface_coef,
    cons_node,
    cons_count,
    relay,
    rows_in,
    rows,
    faces_out,
    faces_in,
    m_nodes,
    a_nodes,
    m_pipes,
    a_pipes,
    f_nodes,
    f_faces,
    inner,
    outer,
    node,
    serves,
    high,
    low,
    pipe_high,
    pipe_low,
    face_high,
    face_low,
    extra_high,
    extra_low,
    mixed_both,
    rho,
    delta,
    step,
    resid,
    load_sem,
    out_sem,
    relay_send,
    relay_recv,
    rows_send,
    rows_self_send,
    rows_recv,
    face_send,
    face_recv,
):
    rank = lax.axis_index("dom")
    core = lax.axis_index("samp")
    owner_half = rank // HALF_DOM
    left = slice(0, WIDTH)
    right = slice(WIDTH, 2 * WIDTH)

    at_y, at_z, at_x = rank // 32, lax.rem(rank // REACH, DEEP), lax.rem(rank, REACH)

    def place(y, z, x):
        return 32 * y + REACH * z + x

    barrier = pltpu.get_barrier_semaphore()
    around = [lax.rem(rank + o + N_DOM, N_DOM) for o in (1, -1, REACH, -REACH)]
    for dz in FAR_FIRST_Z[:-1]:
        pl.semaphore_signal(
            barrier,
            inc=1,
            device_id=(place(at_y, lax.rem(at_z + dz, DEEP), at_x), core),
            device_id_type=MESH,
        )
    for dx in FAR_FIRST_X:
        for y in range(2):
            for c in range(2):
                source = place(2 * core + y, at_z, lax.rem(at_x + dx, REACH))
                pl.semaphore_signal(barrier, inc=1, device_id=(source, c), device_id_type=MESH)
    for q in around:
        pl.semaphore_signal(barrier, inc=1, device_id=(q, core), device_id_type=MESH)

    loads = [
        (iface_node_hbm, iface_node),
        (state_hbm, state),
        (demand_hbm, demand),
        (node_coef_hbm, node_coef),
        (pipe_ends_hbm, pipe_ends),
        (pipe_coef_hbm, pipe_coef),
        (cons_node_hbm, cons_node),
        (cons_count_hbm, cons_count),
        (iface_coef_hbm, iface_coef),
    ]
    loads = [
        pltpu.make_async_copy(src, dst, load_sem.at[i]) for i, (src, dst) in enumerate(loads)
    ]
    for load in loads:
        load.start()

    def chunk(i, size):
        return slice(i * size, (i + 1) * size)

    loads[0].wait()
    face_rows = [iface_node[0, c : c + 1, :].astype(F32) for c in range(4)]
    lane_of_node = lax.broadcasted_iota(jnp.int32, (IFACE, WIDTH), 1).astype(F32)
    for c in range(4):
        ids = column(face_rows[c])
        for part in range(NODES // WIDTH):
            f_faces[chunk(c, IFACE), chunk(part, WIDTH)] = onehot(
                ids == lane_of_node + float(part * WIDTH)
            ).astype(BF16)
    loads[1].wait()
    for i in range(2):
        for f in range(2):
            high[chunk(i, 128), chunk(f, WIDTH)], low[chunk(i, 128), chunk(f, WIDTH)] = split(
                state[f, chunk(i, 128), :]
            )

    def face_copies(turn):
        return [
            pltpu.make_async_remote_copy(
                src_ref=faces_out.at[turn, c],
                dst_ref=faces_in.at[turn, PARTNER_COLOUR[c]],
                send_sem=face_send.at[turn, c],
                recv_sem=face_recv.at[turn, PARTNER_COLOUR[c]],
                device_id=(around[c], core),
                device_id_type=MESH,
            )
            for c in range(4)
        ]

    def face_values(turn, c):
        table = f_faces[chunk(c, IFACE), :]
        faces_out[turn, c] = mm(table, high[...]) + mm(table, low[...])

    def pipe_drops(i):
        at = chunk(i, 128)
        drops = mm(m_pipes[at, :], high[...]) + mm(m_pipes[at, :], low[...])
        sums = mm(a_pipes[at, :], two(high[:, right], low[:, right]))
        return drops[:, left], drops[:, right], sums[:, left] + sums[:, right]

    copies = face_copies(0)
    for c in range(4):
        face_values(0, c)
    loads[2].wait()
    pl.semaphore_wait(barrier, DEEP - 1 + 16 + 4)

    def rows_of(y, z):
        return demand.at[0, :, pl.ds(pl.multiple_of(place(y, z, 0) * SLOTS, SLOTS), REACH * SLOTS)]

    for dz in FAR_FIRST_Z[:-1]:
        z = lax.rem(at_z + dz, DEEP)
        for y in range(4):
            pltpu.make_async_remote_copy(
                src_ref=rows_of(y, z),
                dst_ref=relay.at[at_z, y],
                send_sem=relay_send,
                recv_sem=relay_recv,
                device_id=(place(at_y, z, at_x), core),
                device_id_type=MESH,
            ).start()
    for y in range(4):
        pltpu.make_async_copy(rows_of(y, at_z), relay.at[at_z, y], relay_recv).start()

    for load in loads[3:]:
        load.wait()

    for i in range(NODES // 128):
        node_of_row = lax.broadcasted_iota(jnp.int32, (128, PIPES), 0) + i * 128
        at_start = onehot(pipe_ends[0:1, :] == node_of_row)
        at_end = onehot(pipe_ends[1:2, :] == node_of_row)
        m_nodes[chunk(i, 128), :] = (at_start - at_end).astype(BF16)
        a_nodes[chunk(i, 128), :] = (at_start + at_end).astype(BF16)
    lane_of_node = lax.broadcasted_iota(jnp.int32, (128, WIDTH), 1).astype(F32)
    for i in range(PIPES // 128):
        start_ids = column(pipe_ends[0:1, chunk(i, 128)].astype(F32))
        end_ids = column(pipe_ends[1:2, chunk(i, 128)].astype(F32))
        for part in range(NODES // WIDTH):
            at_start = onehot(start_ids == lane_of_node + float(part * WIDTH))
            at_end = onehot(end_ids == lane_of_node + float(part * WIDTH))
            m_pipes[chunk(i, 128), chunk(part, WIDTH)] = (at_start - at_end).astype(BF16)
            a_pipes[chunk(i, 128), chunk(part, WIDTH)] = (at_start + at_end).astype(BF16)
    face_ids = jnp.concatenate(face_rows, axis=1)
    for i in range(NODES // 128):
        node_of_row = lax.broadcasted_iota(jnp.int32, (128, FACES), 0) + i * 128
        f_nodes[chunk(i, 128), :] = onehot(face_ids == node_of_row.astype(F32)).astype(BF16)

    def scatter(table, i, upper, lower):
        return mm(table[chunk(i, 128), :], upper[...]) + mm(table[chunk(i, 128), :], lower[...])

    for copy in copies:
        copy.start()

    for i in range(PIPES // 128):
        at = chunk(i, 128)
        drop, temp_drop, temp_sum = pipe_drops(i)
        flow, heat, slope, mixed, half_flow, mixing = pipe_terms(
            drop, temp_sum, temp_drop, column(pipe_coef[0:1, at]), column(pipe_coef[1:2, at])
        )
        inner[0, at], inner[1, at], inner[2, at], inner[3, at] = slope, mixed, half_flow, mixing
        pipe_high[at, left], pipe_low[at, left] = split(flow)
        pipe_high[at, right], pipe_low[at, right] = split(heat)
        extra_high[at, left], extra_low[at, left] = split(slope)
        extra_high[at, right], extra_low[at, right] = split(mixing)
        mixed_both[at, left], mixed_both[at, right] = split(mixed)
    for i in range(NODES // 128):
        at = chunk(i, 128)
        rho[at, :] = scatter(m_nodes, i, pipe_high, pipe_low)
        slopes = scatter(a_nodes, i, extra_high, extra_low)
        cross = mm(a_nodes[at, :], mixed_both[...])
        node[0, at] = column(node_coef[0:1, at])
        node[1, at] = column(node_coef[1:2, at])
        node[2, at] = node[0, at] + slopes[:, left]
        node[3, at] = 0.5 * rho[at, left] + slopes[:, right]
        node[4, at] = cross[:, left] + cross[:, right]
        live = lax.broadcasted_iota(jnp.int32, (128, 2 * SLOTS), 1) < cons_count[...]
        here = cons_node[...] == lax.broadcasted_iota(jnp.int32, (128, 2 * SLOTS), 0) + i * 128
        serves[at, :] = onehot(jnp.logical_and(live, here)).astype(BF16)

    step[...] = jnp.zeros_like(step)

    lane = lax.broadcasted_iota(jnp.int32, (IFACE, N_DOM), 1)

    def iface_column(which, c):
        owner = (rank, around[1], rank, around[3])[c]
        mine = jnp.where(lane == owner, iface_coef[which, c // 2], F32(0.0))
        return jnp.broadcast_to(jnp.sum(mine, axis=1, keepdims=True), (IFACE, WIDTH))

    for c in range(4):
        outer[0, chunk(c, IFACE)] = iface_column(0, c)
        outer[1, chunk(c, IFACE)] = iface_column(1, c)
    pltpu.make_async_remote_copy(
        src_ref=relay,
        dst_ref=relay,
        send_sem=relay_send,
        recv_sem=relay_recv,
        device_id=(rank, 1 - core),
        device_id_type=MESH,
    ).wait_recv()
    group = core * 8 + lax.rem(at_y, 2) * REACH + at_x

    def relayed(y, x):
        return relay.at[:, y, :, pl.ds(pl.multiple_of(x * SLOTS, SLOTS), SLOTS)]

    for dy in FAR_FIRST_X:
        for dx in FAR_FIRST_X:
            if (dy, dx) != (0, 0):
                y, x = lax.rem(at_y + dy, 4), lax.rem(at_x + dx, REACH)
                pltpu.make_async_remote_copy(
                    src_ref=relayed(y, x),
                    dst_ref=rows_in.at[group],
                    send_sem=rows_send,
                    recv_sem=rows_recv,
                    device_id=(place(y, at_z, x), owner_half),
                    device_id_type=MESH,
                ).start()
    own_rows = relayed(at_y, at_x)

    @pl.when(owner_half == core)
    def _():
        pltpu.make_async_copy(own_rows, rows_in.at[group], rows_recv).start()

    across = pltpu.make_async_remote_copy(
        src_ref=own_rows,
        dst_ref=rows_in.at[group],
        send_sem=rows_self_send,
        recv_sem=rows_recv,
        device_id=(rank, 1 - core),
        device_id_type=MESH,
    )

    @pl.when(owner_half != core)
    def _():
        across.start()

    for copy in copies:
        copy.wait_recv()
    for c in range(4):
        at = chunk(c, IFACE)
        near_head, near_temp = faces_out[0, c, :, left], faces_out[0, c, :, right]
        far_head, far_temp = faces_in[0, c, :, left], faces_in[0, c, :, right]
        flow, heat, slope, mixed, half_flow, mixing = pipe_terms(
            near_head - far_head, near_temp + far_temp, near_temp - far_temp, outer[0, at], outer[1, at]
        )
        upper = half_flow + mixing
        outer[0, at], outer[1, at], outer[2, at], outer[3, at] = slope, mixed, upper, half_flow - mixing
        face_high[at, left], face_low[at, left] = split(flow)
        face_high[at, right], face_low[at, right] = split(heat)
        extra_high[at, left], extra_low[at, left] = split(slope)
        extra_high[at, right], extra_low[at, right] = split(upper)
        mixed_both[at, left], mixed_both[at, right] = split(mixed)
    for i in range(NODES // 128):
        at = chunk(i, 128)
        rho[at, :] += scatter(f_nodes, i, face_high, face_low)
        table = f_nodes[at, :]
        slopes = mm(table, extra_high[:FACES, :]) + mm(table, extra_low[:FACES, :])
        cross = mm(table, mixed_both[:FACES, :])
        node[2, at] = 1.0 / (node[2, at] + slopes[:, left])
        node[3, at] += slopes[:, right]
        node[4, at] += cross[:, left] + cross[:, right]

    def precondition(i):
        at = chunk(i, 128)
        head = -rho[at, left] * node[2, at]
        temp = -(rho[at, right] + node[4, at] * head) * node[3, at]
        delta[at, left] = head
        delta[at, right] = temp
        high[at, left], low[at, left] = split(head)
        high[at, right], low[at, right] = split(temp)

    pltpu.make_async_remote_copy(
        src_ref=rows_in,
        dst_ref=rows_in,
        send_sem=rows_send,
        recv_sem=rows_recv,
        device_id=(rank, 1 - core),
        device_id_type=MESH,
    ).wait_recv()
    for h in range(2):
        for y in range(2):
            for z in range(DEEP):
                for x in range(REACH):
                    rows[chunk(place(y, z, x), 2), chunk(h, SLOTS)] = rows_in[
                        h * 8 + y * REACH + x, z
                    ].astype(F32)
    for i in range(NODES // 128):
        at = chunk(i, 128)
        usage = lax.dot_general(
            serves[at, :],
            rows[...].astype(BF16),
            (((1,), (1,)), ((), ())),
            preferred_element_type=F32,
        )
        cooling = node[1, at] + usage
        node[1, at] = cooling
        node[3, at] = 1.0 / (node[3, at] + cooling)
        rho[at, left] += node[0, at] * state[0, at] + usage
        rho[at, right] += cooling * state[1, at]
        resid[0, at] = rho[at, left]
        resid[1, at] = rho[at, right]
        precondition(i)

    resid_out = pltpu.make_async_copy(resid, resid_hbm, out_sem.at[0])
    resid_out.start()

    wraps_x = (at_x == 0).astype(jnp.int32)
    wraps_z = (at_z == 0).astype(jnp.int32)
    leaving = [
        (colour, lax.rem(rank + (1 - 2 * lax.rem(colour, 2)) * reach + N_DOM, N_DOM))
        for colour, reach in (
            (wraps_x, 1),
            (2 + wraps_z, REACH),
            (1 - wraps_x, 1),
            (3 - wraps_z, REACH),
        )
    ]

    def one_turn(turn, carry):
        copies = face_copies(turn)
        for colour, target in leaving:
            table = f_faces[pl.ds(pl.multiple_of(colour * IFACE, IFACE), IFACE), :]
            faces_out[turn, colour] = mm(table, high[...]) + mm(table, low[...])
            pltpu.make_async_remote_copy(
                src_ref=faces_out.at[turn, colour],
                dst_ref=faces_in.at[turn, colour + 1 - 2 * lax.rem(colour, 2)],
                send_sem=face_send.at[turn, colour],
                recv_sem=face_recv.at[turn, colour + 1 - 2 * lax.rem(colour, 2)],
                device_id=(target, core),
                device_id_type=MESH,
            ).start()
        for i in range(PIPES // 128):
            at = chunk(i, 128)
            drop, temp_drop, temp_sum = pipe_drops(i)
            pipe_high[at, left], pipe_low[at, left] = split(inner[0, at] * drop)
            pipe_high[at, right], pipe_low[at, right] = split(
                inner[1, at] * drop + inner[2, at] * temp_sum + inner[3, at] * temp_drop
            )
        for c in range(4):
            at = chunk(c, IFACE)
            head, temp = faces_out[turn, c, :, left], faces_out[turn, c, :, right]
            face_high[at, left], face_low[at, left] = split(outer[0, at] * head)
            face_high[at, right], face_low[at, right] = split(outer[1, at] * head + outer[2, at] * temp)
        for i in range(NODES // 128):
            at = chunk(i, 128)
            moved = scatter(m_nodes, i, pipe_high, pipe_low) + scatter(f_nodes, i, face_high, face_low)
            head, temp = delta[at, left], delta[at, right]
            rho[at, left] += moved[:, left] + node[0, at] * head
            rho[at, right] += moved[:, right] + node[1, at] * temp
            step[0, at] += head
            step[1, at] += temp
        for copy in copies:
            copy.wait_recv()
        for c in range(4):
            at = chunk(c, IFACE)
            head, temp = faces_in[turn, c, :, left], faces_in[turn, c, :, right]
            face_high[at, left], face_low[at, left] = split(-outer[0, at] * head)
            face_high[at, right], face_low[at, right] = split(outer[3, at] * temp - outer[1, at] * head)
        for i in range(NODES // 128):
            at = chunk(i, 128)
            rho[at, :] += scatter(f_nodes, i, face_high, face_low)
            precondition(i)
        return carry

    lax.fori_loop(1, ITERS + 1, one_turn, 0)
    for i in range(NODES // 128):
        at = chunk(i, 128)
        step[0, at] += delta[at, left]
        step[1, at] += delta[at, right]
    step_out = pltpu.make_async_copy(step, step_hbm, out_sem.at[1])
    step_out.start()

    def sent(turn, carry):
        for copy in face_copies(turn):
            copy.wait_send()
        return carry

    lax.fori_loop(0, ITERS + 1, sent, 0)
    pltpu.make_async_remote_copy(
        src_ref=relay.at[pl.ds(0, DEEP - 1)],
        dst_ref=relay.at[pl.ds(0, DEEP - 1)],
        send_sem=relay_send,
        recv_sem=relay_recv,
        device_id=(rank, 1 - core),
        device_id_type=MESH,
    ).wait_send()
    pltpu.make_async_remote_copy(
        src_ref=rows_in.at[pl.ds(0, 15)],
        dst_ref=rows_in.at[pl.ds(0, 15)],
        send_sem=rows_send,
        recv_sem=rows_recv,
        device_id=(rank, 1 - core),
        device_id_type=MESH,
    ).wait_send()

    @pl.when(owner_half != core)
    def _():
        across.wait_send()

    resid_out.wait()
    step_out.wait()


def write_out(step_in, resid_in, step_out, resid_out, stage, in_sem, out_sem):
    pairs = [(resid_in, resid_out, 0), (resid_in, resid_out, 1), (step_in, step_out, 0), (step_in, step_out, 1)]
    fetches = [
        pltpu.make_async_copy(src.at[f], stage.at[i], in_sem.at[i])
        for i, (src, _, f) in enumerate(pairs)
    ]
    stores = [
        pltpu.make_async_copy(stage.at[i], dst.at[f], out_sem.at[i])
        for i, (_, dst, f) in enumerate(pairs)
    ]
    for fetch in fetches:
        fetch.start()
    for fetch, store in zip(fetches, stores):
        fetch.wait()
        store.start()
    for store in stores:
        store.wait()


def shards(
    state,
    demand_load,
    node_coef,
    pipe_ends,
    pipe_coef,
    iface_node,
    iface_coef,
    cons_node,
    cons_count,
):
    vmem = pltpu.VMEM
    dma = pltpu.SemaphoreType.DMA
    anywhere = pl.BlockSpec(memory_space=pl.ANY)
    out = jax.ShapeDtypeStruct((2, NODES, WIDTH), F32)
    step, resid = pl.pallas_call(
        kernel,
        out_shape=(out, out),
        in_specs=[anywhere] * 9,
        out_specs=(anywhere, anywhere),
        scratch_shapes=[
            vmem((2, NODES, WIDTH), F32),
            vmem((1, 2, N_DOM * SLOTS), BF16),
            vmem((2, NODES), F32),
            vmem((2, PIPES), jnp.int32),
            vmem((2, PIPES), F32),
            vmem((1, 4, IFACE), jnp.int32),
            vmem((2, 2, IFACE, N_DOM), F32),
            vmem((1, 2 * SLOTS), jnp.int32),
            vmem((1, 1), jnp.int32),
            vmem((DEEP, 4, 2, REACH * SLOTS), BF16),
            vmem((16, DEEP, 2, SLOTS), BF16),
            vmem((WIDTH, 2 * SLOTS), F32),
            vmem((ITERS + 1, 4, IFACE, 2 * WIDTH), F32),
            vmem((ITERS + 1, 4, IFACE, 2 * WIDTH), F32),
            vmem((NODES, PIPES), BF16),
            vmem((NODES, PIPES), BF16),
            vmem((PIPES, NODES), BF16),
            vmem((PIPES, NODES), BF16),
            vmem((NODES, FACES), BF16),
            vmem((FACES, NODES), BF16),
            vmem((4, PIPES, WIDTH), F32),
            vmem((4, FACES, WIDTH), F32),
            vmem((5, NODES, WIDTH), F32),
            vmem((NODES, 2 * SLOTS), BF16),
            vmem((NODES, 2 * WIDTH), BF16),
            vmem((NODES, 2 * WIDTH), BF16),
            vmem((PIPES, 2 * WIDTH), BF16),
            vmem((PIPES, 2 * WIDTH), BF16),
            vmem((FACES, 2 * WIDTH), BF16),
            vmem((FACES, 2 * WIDTH), BF16),
            vmem((PIPES, 2 * WIDTH), BF16),
            vmem((PIPES, 2 * WIDTH), BF16),
            vmem((PIPES, 2 * WIDTH), BF16),
            vmem((NODES, 2 * WIDTH), F32),
            vmem((NODES, 2 * WIDTH), F32),
            vmem((2, NODES, WIDTH), F32),
            vmem((2, NODES, WIDTH), F32),
            dma((9,)),
            dma((2,)),
            dma,
            dma,
            dma,
            dma,
            dma,
            dma((ITERS + 1, 4)),
            dma((ITERS + 1, 4)),
        ],
        compiler_params=pltpu.CompilerParams(
            collective_id=0, has_side_effects=True, vmem_limit_bytes=56 << 20
        ),
        name="newton_step",
    )(
        state,
        demand_load,
        node_coef,
        pipe_ends,
        pipe_coef,
        iface_node,
        jnp.transpose(iface_coef, (0, 2, 3, 1)),
        cons_node,
        cons_count.reshape(1, 1),
    )
    step, resid = pl.pallas_call(
        write_out,
        out_shape=(out, out),
        in_specs=[anywhere] * 2,
        out_specs=(anywhere, anywhere),
        scratch_shapes=[
            vmem((4, NODES, WIDTH), F32),
            dma((4,)),
            dma((4,)),
        ],
        compiler_params=pltpu.CompilerParams(vmem_limit_bytes=56 << 20),
        name="write_out",
    )(step, resid)
    return step, resid


def solution(mesh):
    placed = (
        P(None, "dom", "samp"),
        P("samp", "dom", None),
        P(None, "dom"),
        P(None, "dom"),
        P(None, "dom"),
        P("dom", None, None),
        P(),
        P("dom", None),
        P("dom"),
    )
    return jax.shard_map(
        shards,
        mesh=mesh,
        in_specs=placed,
        out_specs=(P(None, "dom", "samp"), P(None, "dom", "samp")),
        check_vma=False,
    )
```
